256 devices in a mesh: dp: 2 (over z_lo), wide: 32 (over x, y, core), mlp: 4 (over z_hi).
Axes of the slice: x: 4, y: 4, z: 8 (z_hi: 4, z_lo: 2; z = z_hi * 2 + z_lo), core: 2. Of those that a mesh axis runs over, the one named last changes fastest.
Arguments:
- inputs: bfloat16 [8, 96, 180, 768], P('dp', 'wide', 'mlp'), may hold values from -6 to 6
- validity: int32 [8, 96, 180], P('dp', 'wide', 'mlp'), may hold values from 0 to 1, as said below
- gain_first: float32 [768], replicated, may hold values from 0.5 to 1.5
- shift_first: float32 [768], replicated, may hold values from -3 to 3
- spectral_in: bfloat16 [2, 8, 96, 96], P(None, 'mlp'), may hold values from -0.4375 to 0.4375
- spectral_in_bias: float32 [2, 8, 96], P(None, 'mlp'), may hold values from -3 to 3
- spectral_out: bfloat16 [2, 8, 96, 96], P(None, 'mlp'), may hold values from -0.15625 to 0.15625
- spectral_out_bias: float32 [2, 8, 96], P(None, 'mlp'), may hold values from -0.6 to 0.6
- gain_second: float32 [768], replicated, may hold values from 0.5 to 1.5
- shift_second: float32 [768], replicated, may hold values from -3 to 3
- weight_in: bfloat16 [768, 3072], P(None, 'mlp'), may hold values from -0.21875 to 0.21875
- bias_in: float32 [3072], P('mlp'), may hold values from -3 to 3
- weight_out: bfloat16 [3072, 768], P('mlp'), may hold values from -0.21875 to 0.21875
- bias_out: float32 [768], replicated, may hold values from -3 to 3
- cotangent: bfloat16 [8, 96, 180, 768], P('dp', 'wide', 'mlp'), may hold values from -6 to 6
Outputs:
- output: bfloat16 [8, 96, 180, 768], P('dp', 'wide', 'mlp')
- grad_inputs: float32 [8, 96, 180, 768], P('dp', 'wide', 'mlp')
- grad_gain_first: float32 [768], P('mlp')
- grad_shift_first: float32 [768], P('mlp')
- grad_spectral_in: float32 [2, 8, 96, 96], replicated
- grad_spectral_in_bias: float32 [2, 8, 96], replicated
- grad_spectral_out: float32 [2, 8, 96, 96], replicated
- grad_spectral_out_bias: float32 [2, 8, 96], replicated
- grad_gain_second: float32 [768], P('mlp')
- grad_shift_second: float32 [768], P('mlp')
- grad_weight_in: float32 [768, 3072], P(None, 'mlp')
- grad_bias_in: float32 [3072], P('mlp')
- grad_weight_out: float32 [3072, 768], P('mlp')
- grad_bias_out: float32 [768], P('mlp')
The draws below stay inside these ranges and needn't reach their ends.
Inputs may be any that keep to these rules, and one draw needn't show every extreme that they name: `validity`: 1 marks a present patch; the last 6 latitude rows of every snapshot are 0.
All inputs are finite; a program needn't handle non-finite values.
Results may differ from the reference program's by a relative error of at most 0.018.
The reference program's roundings to bfloat16 on the way count: a program that leaves them out, or rounds other values in their place, can miss the bound.
Values may be sent and summed in bfloat16 or wider, within the bound.
No kernel may reach another device: no remote copies, remote signals or barrier semaphores. Data moves between devices by JAX's collectives and lax.ppermute only.
A program may use at most 192 MiB of HBM per device.

```python
import math
import jax
import jax.numpy as jnp
from jax import lax

D = 768
FF = 3072
NB = 8
W = 180
H = 96
KWP = 96
BS = 96
SNAPS = 8
N_MLP = 4


def draw_validity(key, part):
    key = jax.random.fold_in(key, 11)
    levels = jax.random.randint(key, (SNAPS, H, W), 0, 8)
    latitude = jnp.arange(H, dtype=jnp.int32)[None, :, None]
    return jnp.where((levels < 7) & (latitude < H - H // 16), 1, 0).astype(jnp.int32)


def level_of(key, extent, pieces, least, largest):
    loudness = 1.0
    for axis_at, blocks in pieces:
        steps = jax.random.uniform(jax.random.fold_in(jax.random.fold_in(key, 6), axis_at), (blocks,), jnp.float32, least / len(pieces), largest / len(pieces))
        loudness = loudness * jnp.repeat(jnp.exp(steps), extent[axis_at] // blocks).reshape((-1,) + (1,) * (len(extent) - 1 - axis_at))
    return loudness


def gaussian(stream_key, extent, scale, most, split=(), kind=jnp.bfloat16):
    factor_of = level_of(stream_key, extent, split, -0.22, 0.18) if split else 1.0
    entries = jax.random.normal(stream_key, extent, jnp.float32) * scale * factor_of
    return jnp.minimum(jnp.maximum(entries, -most), most).astype(kind)


def setup_inputs(seed: int = 0) -> dict:
    key_of = jax.random.split(jax.random.key(seed), 16)
    return {
        "inputs": gaussian(key_of[0], (SNAPS, H, W, D), 1.0, 6.0, ((0, 2), (1, 32), (2, 4))),
        "validity": draw_validity(jax.random.fold_in(key_of[15], 71), 0),
        "gain_first": jnp.clip(1.0 + 0.1 * jax.random.normal(key_of[2], (D,), jnp.float32), 0.5, 1.5),
        "shift_first": gaussian(key_of[3], (D,), 0.5, 3.0, (), jnp.float32),
        "spectral_in": gaussian(key_of[4], (2, NB, BS, BS), (2 * BS) ** -0.5, 0.4375, ((1, 4),)),
        "spectral_in_bias": gaussian(key_of[5], (2, NB, BS), 0.5, 3.0, ((1, 4),), jnp.float32),
        "spectral_out": gaussian(key_of[6], (2, NB, BS, BS), (18 * BS) ** -0.5, 0.15625, ((1, 4),)),
        "spectral_out_bias": gaussian(key_of[7], (2, NB, BS), 0.15, 0.6, ((1, 4),), jnp.float32),
        "gain_second": jnp.clip(1.0 + 0.1 * jax.random.normal(key_of[8], (D,), jnp.float32), 0.5, 1.5),
        "shift_second": gaussian(key_of[9], (D,), 0.5, 3.0, (), jnp.float32),
        "weight_in": gaussian(key_of[10], (D, FF), D ** -0.5, 0.21875, ((1, 4),)),
        "bias_in": gaussian(key_of[11], (FF,), 0.5, 3.0, ((0, 4),), jnp.float32),
        "weight_out": gaussian(key_of[12], (FF, D), (FF // 4) ** -0.5, 0.21875, ((0, 4),)),
        "bias_out": gaussian(key_of[13], (D,), 0.5, 3.0, (), jnp.float32),
        "cotangent": gaussian(key_of[14], (SNAPS, H, W, D), 1.0, 6.0, ((0, 2), (1, 32), (2, 4))),
    }


EPSILON = 1e-05
SHRINK = 0.01

@jax.custom_vjp
def low(v):
    return lax.optimization_barrier(v.astype(jnp.bfloat16)).astype(jnp.float32)

@jax.custom_vjp
def low_back(v):
    return v

def low_keep(v):
    return (low(v), None)

def low_pass(kept, grad):
    return (grad,)

def back_keep(v):
    return (v, None)

def back_low(kept, grad):
    return (low(grad),)
low.defvjp(low_keep, low_pass)
low_back.defvjp(back_keep, back_low)

def longitude_tables(length, columns):
    index = jnp.arange(length, dtype=jnp.int32)
    order = jnp.arange(columns, dtype=jnp.int32)
    phase_angle = (index[:, None] * order[None, :] % length).astype(jnp.float32) * (2.0 * math.pi / length)
    live_scale = jnp.where(order < length // 2 + 1, 1.0 / math.sqrt(length), 0.0).astype(jnp.float32)
    weight = jnp.where((order == 0) | (2 * order == length), 1.0, 2.0).astype(jnp.float32) * live_scale
    forward = jnp.stack([jnp.cos(phase_angle) * live_scale[None, :], -jnp.sin(phase_angle) * live_scale[None, :]], axis=1)
    inverse = jnp.stack([jnp.cos(phase_angle).T * weight[:, None], -jnp.sin(phase_angle).T * weight[:, None]], axis=0)
    return (forward, inverse)

def latitude_tables(length):
    index = jnp.arange(length, dtype=jnp.int32)
    phase_angle = (index[:, None] * index[None, :] % length).astype(jnp.float32) * (2.0 * math.pi / length)
    cosine = jnp.cos(phase_angle) / math.sqrt(length)
    sine_part = jnp.sin(phase_angle) / math.sqrt(length)
    forward = jnp.stack([jnp.stack([cosine, sine_part], axis=1), jnp.stack([-sine_part, cosine], axis=1)], axis=0)
    inverse = jnp.stack([jnp.stack([cosine, -sine_part], axis=1), jnp.stack([sine_part, cosine], axis=1)], axis=0)
    return (forward, inverse)

def real_form(weights):
    real_part = weights[0]
    imag_part = weights[1]
    upper_rows = jnp.stack([real_part, imag_part], axis=2)
    bottom = jnp.stack([-imag_part, real_part], axis=2)
    return jnp.stack([upper_rows, bottom], axis=1)

def shrink(value):
    return value - SHRINK * value * lax.rsqrt(value * value + SHRINK * SHRINK)

def layer_norm(values):
    centred = values - lax.optimization_barrier(jnp.mean(values, axis=-1, keepdims=True))
    return centred * lax.rsqrt(lax.optimization_barrier(jnp.mean(centred * centred, axis=-1, keepdims=True)) + EPSILON)

def layer(params, snapshot, present, tables):
    gain_first, shift_first, spectral_in, spectral_in_bias, spectral_out, spectral_out_bias, gain_second, shift_second, weight_in, bias_in, weight_out, bias_out = params
    lon_fwd, lon_inv, lat_fwd, lat_inv = tables
    highest = lax.Precision.HIGHEST
    normed_first = layer_norm(snapshot)
    masked = (normed_first * gain_first + shift_first) * present[..., None]
    spectrum = low_back(low(jnp.einsum('hwc,wpk->hpkc', low(masked), lon_fwd, precision=highest)))
    grid_low = low(low_back(jnp.einsum('pjqh,hqkc->jpkc', lat_fwd, spectrum, precision=highest)))
    blocks = grid_low.reshape(H, 2, KWP, NB, BS)
    first_layer = low_back(jnp.einsum('jqkbe,bqepf->jpkbf', blocks, real_form(spectral_in), precision=highest)) + spectral_in_bias[None, :, None, :, :]
    active = low(jax.nn.gelu(first_layer, approximate=False))
    second = low_back(jnp.einsum('jqkbe,bqepf->jpkbf', active, real_form(spectral_out), precision=highest)) + spectral_out_bias[None, :, None, :, :]
    shrunk = low(shrink(second)).reshape(H, 2, KWP, D)
    back_rows = low_back(low(jnp.einsum('pjqh,hqkc->jpkc', lat_inv, shrunk, precision=highest)))
    filtered = low_back(jnp.einsum('hpkc,pkw->hwc', back_rows, lon_inv, precision=highest))
    stream = snapshot + filtered + masked
    normed_second = layer_norm(low(stream))
    token_rows = low(normed_second * gain_second + shift_second).reshape(H * W, D)
    group_size = FF // N_MLP
    branch = jnp.zeros((H * W, D), jnp.float32)
    for shard_index in range(N_MLP):
        first_unit = shard_index * group_size
        pre_act = low_back(jnp.dot(low_back(token_rows), weight_in[:, first_unit:first_unit + group_size], precision=highest, preferred_element_type=jnp.float32)) + bias_in[first_unit:first_unit + group_size]
        hidden = low(jax.nn.gelu(pre_act, approximate=False))
        branch = branch + low(jnp.dot(hidden, weight_out[first_unit:first_unit + group_size, :], precision=highest, preferred_element_type=jnp.float32))
    branch = low_back(branch).reshape(H, W, D) + bias_out
    return stream + present[..., None] * branch

def reference(inputs, validity, gain_first, shift_first, spectral_in, spectral_in_bias, spectral_out, spectral_out_bias, gain_second, shift_second, weight_in, bias_in, weight_out, bias_out, cotangent):
    params = tuple((value.astype(jnp.float32) for value in (gain_first, shift_first, spectral_in, spectral_in_bias, spectral_out, spectral_out_bias, gain_second, shift_second, weight_in, bias_in, weight_out, bias_out)))
    lon_fwd, lon_inv = longitude_tables(W, KWP)
    lat_fwd, lat_inv = latitude_tables(H)
    tables = (low(lon_fwd), low(lon_inv), low(lat_fwd), low(lat_inv))

    def visit(totals, step_item):
        snapshot, mask_row, seed_grad = step_item
        present = mask_row.astype(jnp.float32)
        result, pullback = jax.vjp(lambda weights, field_in: layer(weights, field_in, present, tables), params, snapshot.astype(jnp.float32))
        gradients, grad_field = pullback(seed_grad.astype(jnp.float32))
        totals = jax.tree.map(lambda left, right: left + right, totals, gradients)
        return (totals, (result.astype(jnp.bfloat16), grad_field))
    initial = jax.tree.map(jnp.zeros_like, params)
    totals, (outputs, grad_inputs) = lax.scan(visit, initial, (inputs, validity, cotangent))
    return (outputs, grad_inputs, totals[0], totals[1], totals[2], totals[3], totals[4], totals[5], totals[6], totals[7], totals[8], totals[9], totals[10], totals[11])
```

```python
import math

import jax
import jax.numpy as jnp
import numpy as np
from jax import lax
from jax.sharding import Mesh
from jax.sharding import PartitionSpec as P

H = 96
KWP = 96
W = 180
WPAD = 48
EPSILON = 1e-05
SHRINK = 0.01

XY = ("x", "y")
WIDE = ("x", "y", "core")
PAIR = ("core", "mlp")
ZED = ("dp", "mlp")
EVERY = ("dp", "x", "y", "core", "mlp")
bf16 = jnp.bfloat16
f32 = jnp.float32


def tables():
    w = np.arange(W)
    k = np.arange(KWP)
    phase = 2.0 * np.pi * ((w[:, None] * k[None, :]) % W) / W
    live = np.where(k < W // 2 + 1, 1.0 / math.sqrt(W), 0.0)
    weight = np.where((k == 0) | (2 * k == W), 1.0, 2.0) * live
    fwd = np.stack([np.cos(phase) * live, -np.sin(phase) * live], axis=2)
    inv = np.stack([np.cos(phase) * weight, -np.sin(phase) * weight], axis=2)
    pad = ((0, 0), (0, WPAD - W // 4), (0, 0), (0, 0))
    fwd = np.pad(fwd.reshape(4, W // 4, KWP, 2), pad).reshape(4, WPAD, 16, 6, 2)
    inv = np.pad(inv.reshape(4, W // 4, KWP, 2), pad).reshape(4, WPAD, 16, 6, 2)
    same = np.eye(6).reshape(2, 3, 6)
    lon_fwd = np.einsum("mwqkp,rih->qhkprmiw", fwd, same).reshape(1152, 1152)
    lon_inv = np.einsum("mwqkp,rih->qhkprmiw", inv, same).reshape(1152, 1152)
    h = np.arange(H)
    angle = 2.0 * np.pi * ((h[:, None] * h[None, :]) % H) / H
    cos = np.cos(angle) / math.sqrt(H)
    sin = np.sin(angle) / math.sqrt(H)
    lat_fwd = np.stack([np.stack([cos, sin]), np.stack([-sin, cos])])
    lat_inv = np.stack([np.stack([cos, -sin]), np.stack([sin, cos])])
    kk = np.eye(6)
    grid_fwd = np.einsum(
        "pqjah,kl->pkjahlq", lat_fwd.reshape(2, 2, H, 16, 6), kk
    ).reshape(1152, 1152)
    grid_inv = np.einsum(
        "pqahj,kl->ahkpqlj", lat_inv.reshape(2, 2, 16, 6, H), kk
    ).reshape(1152, 1152)
    return tuple(np.asarray(t, np.float32).astype(bf16) for t in (lon_fwd, lon_inv, grid_fwd, grid_inv))


def shrink(value):
    return value - SHRINK * value * lax.rsqrt(value * value + SHRINK * SHRINK)


def shrink_slope(value):
    inverse_root = lax.rsqrt(value * value + SHRINK * SHRINK)
    return 1.0 - SHRINK * SHRINK * SHRINK * inverse_root * inverse_root * inverse_root


def gelu_exact(value):
    return jax.nn.gelu(value, approximate=False)


def gelu_back(value, grad):
    return jax.vjp(gelu_exact, value)[1](grad)[0]


def mm(left, right):
    return jnp.dot(left, right, preferred_element_type=f32)


def inner_rows(left, right):
    return lax.dot_general(left, right, (((0,), (0,)), ((), ())), preferred_element_type=f32)


def outer_cols(left, right):
    return lax.dot_general(left, right, (((1,), (1,)), ((), ())), preferred_element_type=f32)


def swap(value, axes):
    return lax.all_to_all(value, axes, 0, 0, tiled=True)


def spread(value, axes, count):
    return swap(jnp.broadcast_to(value[None], (count,) + value.shape), axes)


def block_form(weights):
    eye = jnp.eye(4, dtype=weights.dtype)
    dense = jnp.einsum("pbef,bc->pbecf", weights, eye).reshape(2, 384, 384)
    return jnp.concatenate(
        [
            jnp.concatenate([dense[0], dense[1]], axis=1),
            jnp.concatenate([-dense[1], dense[0]], axis=1),
        ],
        axis=0,
    )


def block_grads(grad):
    quad = grad.reshape(2, 384, 2, 384)
    real = quad[0, :, 0] + quad[1, :, 1]
    imag = quad[0, :, 1] - quad[1, :, 0]
    both = jnp.stack([real, imag])
    return jnp.stack([both[:, 96 * b : 96 * b + 96, 96 * b : 96 * b + 96] for b in range(4)], axis=1)


def pack(tokens):
    halves = jnp.stack([tokens[..., :384], tokens[..., 384:]])
    return swap(halves.reshape(8, 144, 384), PAIR).reshape(1152, 384)


def unpack(rows):
    back = swap(rows.reshape(8, 144, 384), PAIR).reshape(2, 4, 3, WPAD, 384)
    return jnp.concatenate([back[0], back[1]], axis=-1)


def across(rows):
    return swap(rows.reshape(16, 72, 384), XY).reshape(1152, 384)


def lanes(rows):
    return jnp.concatenate([rows[:576], rows[576:]], axis=1)


def unlanes(wide_rows):
    return jnp.concatenate([wide_rows[:, :384], wide_rows[:, 384:]], axis=0)


def shards(
    inputs,
    validity,
    gain_first,
    shift_first,
    spectral_in,
    spectral_in_bias,
    spectral_out,
    spectral_out_bias,
    gain_second,
    shift_second,
    weight_in,
    bias_in,
    weight_out,
    bias_out,
    cotangent,
):
    half = lax.axis_index("core")
    group = lax.axis_index("mlp")
    wide = lax.axis_index(WIDE)
    lon_fwd, lon_inv, grid_fwd, grid_inv = (jnp.asarray(t) for t in tables())

    both = jnp.concatenate([weight_in, weight_out], axis=0)
    piece = lax.dynamic_slice_in_dim(both, wide * 48, 48, 0)
    parts = spread(
        jnp.concatenate([piece, spectral_in.reshape(48, 768), spectral_out.reshape(48, 768)]),
        "mlp",
        4,
    )
    vectors = spread(
        jnp.concatenate([bias_in, spectral_in_bias.reshape(-1), spectral_out_bias.reshape(-1)]).reshape(
            12, 128
        ),
        "mlp",
        4,
    ).reshape(4, 1536)
    whole = lax.all_gather(parts[:, :48], WIDE)
    w_in = [whole[:16, g].reshape(768, 768) for g in range(4)]
    w_out = [whole[16:, g].reshape(768, 768) for g in range(4)]
    units = vectors[:, :768]

    def my_half(value):
        value = lax.dynamic_slice_in_dim(value, half * 2, 2, 0).swapaxes(0, 1)
        return value.reshape((2, 4) + value.shape[3:])

    mix_in = block_form(my_half(parts[:, 48:96].reshape(4, 2, 2, 96, 96)))
    mix_out = block_form(my_half(parts[:, 96:].reshape(4, 2, 2, 96, 96)))
    mix_in_bias = my_half(vectors[:, 768:1152].reshape(4, 2, 2, 96)).reshape(768)
    mix_out_bias = my_half(vectors[:, 1152:].reshape(4, 2, 2, 96)).reshape(768)

    def widen(value):
        return jnp.pad(value, ((0, 0), (0, 0), (0, WPAD - W // 4), (0, 0)))

    resid = widen(inputs).astype(f32)
    present = widen(validity.astype(f32)[..., None])
    centred_first = resid - jnp.mean(resid, axis=3, keepdims=True)
    scale_first = lax.rsqrt(
        jnp.mean(centred_first * centred_first, axis=3, keepdims=True) + EPSILON
    )
    normed_first = centred_first * scale_first
    masked = (normed_first * gain_first + shift_first) * present

    spectrum = mm(lon_fwd, pack(masked.astype(bf16))).astype(bf16)
    columns = across(spectrum)
    grid_low = lanes(mm(grid_fwd, columns).astype(bf16))
    first_layer = mm(grid_low, mix_in) + mix_in_bias
    active = gelu_exact(first_layer).astype(bf16)
    second = mm(active, mix_out) + mix_out_bias
    shrunk = unlanes(shrink(second).astype(bf16))
    back_low = mm(grid_inv, shrunk).astype(bf16)
    returned = across(back_low)
    filtered = unpack(inner_rows(lon_inv, returned).astype(bf16)).astype(f32)

    stream = resid + filtered + masked
    stream_low = stream.astype(bf16).astype(f32)
    centred = stream_low - jnp.mean(stream_low, axis=3, keepdims=True)
    scale_second = lax.rsqrt(jnp.mean(centred * centred, axis=3, keepdims=True) + EPSILON)
    normed_second = centred * scale_second
    mixed_low = (normed_second * gain_second + shift_second).astype(bf16)
    grad_output = widen(cotangent).astype(f32)
    grad_branch = grad_output * present
    mixed_rows = mixed_low.reshape(576, 768)
    grad_rows = grad_branch.astype(bf16).reshape(576, 768)

    branch = jnp.zeros((576, 768), f32)
    grad_mixed = jnp.zeros((576, 768), f32)
    hidden = []
    grad_pre_low = []
    grad_bias_in = []
    for g in range(4):
        pre_act = mm(mixed_rows, w_in[g]) + units[g]
        grad_pre = gelu_back(pre_act, outer_cols(grad_rows, w_out[g]))
        grad_bias_in.append(jnp.sum(grad_pre, axis=0))
        grad_pre_low.append(grad_pre.astype(bf16))
        grad_mixed = grad_mixed + outer_cols(grad_pre_low[g], w_in[g]).astype(bf16).astype(f32)
        hidden.append(gelu_exact(pre_act).astype(bf16))
        branch = branch + mm(hidden[g], w_out[g]).astype(bf16).astype(f32)
    branch = branch.reshape(4, 3, WPAD, 768) + bias_out
    output = (stream + present * branch).astype(bf16)[:, :, : W // 4]

    grad_bias_out = jnp.sum(grad_branch, axis=(0, 1, 2))
    grad_norm = grad_mixed.reshape(4, 3, WPAD, 768)
    grad_gain_second = jnp.sum(grad_norm * normed_second, axis=(0, 1, 2))
    grad_shift_second = jnp.sum(grad_norm, axis=(0, 1, 2))
    scaled = grad_norm * gain_second
    grad_stream = grad_output + scale_second * (
        scaled
        - jnp.mean(scaled, axis=3, keepdims=True)
        - normed_second * jnp.mean(scaled * normed_second, axis=3, keepdims=True)
    )

    grad_weights = jnp.stack(
        [
            jnp.concatenate(
                [inner_rows(mixed_rows, grad_pre_low[g]), inner_rows(hidden[g], grad_rows)], axis=0
            ).astype(bf16)
            for g in range(4)
        ]
    )
    grad_weights = grad_weights.reshape(4, 32, 48, 768).swapaxes(0, 1).reshape(6144, 768)
    share = lax.psum_scatter(grad_weights, WIDE, scatter_dimension=0, tiled=True)
    share = share.reshape(4, 48, 768)
    share = swap(jnp.concatenate([share, share], axis=0), ZED)
    share = jnp.sum(share.astype(f32), axis=0).astype(bf16)
    grad_slices = lax.all_gather(share, WIDE).reshape(1536, 768).astype(f32)

    def total(vector):
        near = jnp.sum(spread(vector, ("dp", "core", "mlp"), 16), axis=0)
        return jnp.sum(spread(near, XY, 16), axis=0)

    early = total(
        jnp.concatenate(grad_bias_in + [grad_bias_out, grad_gain_second, grad_shift_second]).reshape(
            42, 128
        )
    ).reshape(7, 768)

    grad_back = mm(lon_inv, pack(grad_stream.astype(bf16))).astype(bf16)
    grad_columns = across(grad_back)
    grad_shrunk = lanes(inner_rows(grid_inv, grad_columns))
    grad_second = grad_shrunk * shrink_slope(second)
    grad_second_low = grad_second.astype(bf16)
    grad_first = gelu_back(first_layer, outer_cols(grad_second_low, mix_out))
    grad_first_low = grad_first.astype(bf16)
    grad_grid = unlanes(outer_cols(grad_first_low, mix_in).astype(bf16))
    grad_spectrum = inner_rows(grid_fwd, grad_grid).astype(bf16)
    grad_from_spec = unpack(inner_rows(lon_fwd, across(grad_spectrum)).astype(bf16)).astype(f32)

    grad_filters = jnp.stack(
        [
            block_grads(inner_rows(grid_low, grad_first_low)),
            block_grads(inner_rows(active, grad_second_low)),
        ]
    ).astype(bf16)
    filters = swap(grad_filters.reshape(16, 72, 128), XY)
    filters = jnp.sum(filters.astype(f32), axis=0).astype(bf16)
    filters = jnp.sum(spread(filters, ZED, 8).astype(f32), axis=0).astype(bf16)
    filters = spread(filters, WIDE, 32).reshape(16, 2, 9216).swapaxes(0, 1).astype(f32)
    filters = filters.reshape(2, 2, 2, 4, 96, 96).transpose(1, 2, 0, 3, 4, 5)
    filters = filters.reshape(2, 2, 8, 96, 96)

    grad_normed = (grad_from_spec + grad_stream) * present
    grad_gain_first = jnp.sum(grad_normed * normed_first, axis=(0, 1, 2))
    grad_shift_first = jnp.sum(grad_normed, axis=(0, 1, 2))
    scaled_first = grad_normed * gain_first
    grad_inputs = grad_stream + scale_first * (
        scaled_first
        - jnp.mean(scaled_first, axis=3, keepdims=True)
        - normed_first * jnp.mean(scaled_first * normed_first, axis=3, keepdims=True)
    )
    grad_inputs = grad_inputs[:, :, : W // 4]

    filter_bias = jnp.stack([jnp.sum(grad_first, axis=0), jnp.sum(grad_second, axis=0)])
    filter_bias = filter_bias.reshape(2, 2, 1, 384)
    filter_bias = jnp.where(
        half == jnp.arange(2, dtype=jnp.int32)[None, None, :, None], filter_bias, 0.0
    ).reshape(3072)
    late = total(
        jnp.concatenate([grad_gain_first, grad_shift_first, filter_bias]).reshape(36, 128)
    ).reshape(6, 768)
    filter_bias = late[2:].reshape(2, 2, 8, 96)

    def mine(vector):
        return lax.dynamic_slice_in_dim(vector, group * 192, 192, 0)

    return (
        output,
        grad_inputs,
        mine(late[0]),
        mine(late[1]),
        filters[0],
        filter_bias[0],
        filters[1],
        filter_bias[1],
        mine(early[5]),
        mine(early[6]),
        grad_slices[:768],
        lax.dynamic_slice_in_dim(early[:4], group, 1, 0)[0],
        grad_slices[768:],
        mine(early[4]),
    )


def solution(mesh):
    fine = Mesh(mesh.devices.reshape(2, 4, 4, 2, 4), EVERY)
    tokens = P("dp", WIDE, "mlp")
    placed = (
        tokens,
        tokens,
        P(),
        P(),
        P(None, "mlp"),
        P(None, "mlp"),
        P(None, "mlp"),
        P(None, "mlp"),
        P(),
        P(),
        P(None, "mlp"),
        P("mlp"),
        P("mlp", None),
        P(),
        tokens,
    )
    return jax.shard_map(
        shards,
        mesh=fine,
        in_specs=placed,
        out_specs=(
            tokens,
            tokens,
            P("mlp"),
            P("mlp"),
            P(),
            P(),
            P(),
            P(),
            P("mlp"),
            P("mlp"),
            P(None, "mlp"),
            P("mlp"),
            P("mlp", None),
            P("mlp"),
        ),
        check_vma=False,
    )
```

```python
import math

import jax
import jax.numpy as jnp
import numpy as np
from jax import lax
from jax.experimental import pallas as pl
from jax.experimental.pallas import tpu as pltpu
from jax.sharding import Mesh
from jax.sharding import PartitionSpec as P

H = 96
KWP = 96
W = 180
LON = 45
PAD = 48
EPSILON = 1e-05
SHRINK = 0.01
ROOT_HALF = math.sqrt(0.5)
ROOT_TWO_PI = math.sqrt(2.0 * math.pi)

XY = ("x", "y")
PAIR = ("core", "mlp")
EVERY = ("dp", "x", "y", "core", "mlp")
bf16 = jnp.bfloat16
f32 = jnp.float32
ROOM = pltpu.CompilerParams(vmem_limit_bytes=50 * 1024 * 1024)


def tables():
    w = np.arange(W)
    k = np.arange(KWP)
    phase = 2.0 * np.pi * ((w[:, None] * k[None, :]) % W) / W
    live = np.where(k < W // 2 + 1, 1.0 / math.sqrt(W), 0.0)
    weight = np.where((k == 0) | (2 * k == W), 1.0, 2.0) * live
    fwd = np.stack([np.cos(phase) * live, -np.sin(phase) * live], axis=2)
    inv = np.stack([np.cos(phase) * weight, -np.sin(phase) * weight], axis=2)
    pad = ((0, 0), (0, PAD - LON), (0, 0), (0, 0))
    fwd = np.pad(fwd.reshape(4, LON, KWP, 2), pad).reshape(4, PAD, 16, 6, 2)
    inv = np.pad(inv.reshape(4, LON, KWP, 2), pad).reshape(4, PAD, 16, 6, 2)
    same = np.eye(6).reshape(2, 3, 6)
    lon_fwd = np.einsum("mwqkp,rih->qhkprmiw", fwd, same).reshape(1152, 1152)
    lon_inv = np.einsum("mwqkp,rih->rmiwqhkp", inv, same).reshape(1152, 1152)
    h = np.arange(H)
    angle = 2.0 * np.pi * ((h[:, None] * h[None, :]) % H) / H
    cos = np.cos(angle) / math.sqrt(H)
    sin = np.sin(angle) / math.sqrt(H)
    lat_fwd = np.stack([np.stack([cos, sin]), np.stack([-sin, cos])])
    lat_inv = np.stack([np.stack([cos, -sin]), np.stack([sin, cos])])
    kk = np.eye(6).reshape(2, 3, 6)
    grid_fwd = np.einsum("pqjah,tkl->tpkjahlq", lat_fwd.reshape(2, 2, H, 16, 6), kk)
    grid_inv = np.einsum("pqahj,tkl->tahlpqkj", lat_inv.reshape(2, 2, 16, 6, H), kk)
    grid_fwd = grid_fwd.reshape(2, 576, 1152)
    grid_inv = grid_inv.reshape(2, 1152, 576)

    def low(table):
        return np.ascontiguousarray(table).astype(np.float32).astype(bf16)

    return {
        "lon_fwd": low(lon_fwd),
        "lon_inv": low(lon_inv),
        "lon_fwd_t": low(lon_fwd.T),
        "lon_inv_t": low(lon_inv.T),
        "grid_fwd": low(grid_fwd),
        "grid_inv": low(grid_inv),
        "grid_fwd_t": low(grid_fwd.swapaxes(1, 2)),
        "grid_inv_t": low(grid_inv.swapaxes(1, 2)),
    }


def block_fold():
    at = np.arange(384) // 96
    mask = (at[:, None] == at[None, :]).astype(np.float32)
    fold = np.tile(np.eye(96, 128), (4, 1))
    return mask, fold.astype(np.float32).astype(bf16)


def mm(left, right):
    return jnp.dot(left, right, preferred_element_type=f32)


def inner_rows(left, right):
    return lax.dot_general(left, right, (((0,), (0,)), ((), ())), preferred_element_type=f32)


def outer_cols(left, right):
    return lax.dot_general(left, right, (((1,), (1,)), ((), ())), preferred_element_type=f32)


def gelu_parts(value):
    half = 0.5 * (1.0 + lax.erf(value * ROOT_HALF))
    return half, jnp.exp(-0.5 * value * value) * (1.0 / ROOT_TWO_PI)


def standard(value):
    centred = value - jnp.mean(value, axis=-1, keepdims=True)
    scale = lax.rsqrt(jnp.mean(centred * centred, axis=-1, keepdims=True) + EPSILON)
    return centred * scale, scale


def widen(rows, source):
    for i in range(3):
        rows[PAD * i : PAD * i + LON, :] = source[i].astype(f32)
    return rows[...]


def both_halves(pair, s):
    return jnp.concatenate([pair[0, s], pair[1, s]], axis=-1).astype(f32)


def whole(shape):
    return pl.BlockSpec(shape, lambda *_: (0,) * len(shape))


def struct(shape, dtype):
    return jax.ShapeDtypeStruct(shape, dtype)


def norm_kernel(x, present, gain, shift, out, rows):
    rows[...] = jnp.zeros_like(rows)
    normed, _ = standard(widen(rows, x.at[0]))
    masked = ((normed * gain[...] + shift[...]) * present[...]).astype(bf16)
    out[0, 0] = masked[:, :384]
    out[1, 0] = masked[:, 384:]


def norm_pack(inputs, present, gain, shift):
    return pl.pallas_call(
        norm_kernel,
        grid=(4,),
        in_specs=[
            pl.BlockSpec((1, 3, LON, 768), lambda s: (s, 0, 0, 0)),
            pl.BlockSpec((144, 1), lambda s: (s, 0)),
            whole((1, 768)),
            whole((1, 768)),
        ],
        out_specs=pl.BlockSpec((2, 1, 144, 384), lambda s: (0, s, 0, 0)),
        out_shape=struct((2, 4, 144, 384), bf16),
        scratch_shapes=[pltpu.VMEM((144, 768), f32)],
        compiler_params=ROOM,
    )(inputs, present, gain, shift)


def table_kernel(table, rows, out):
    out[...] = mm(table[...], rows[...]).astype(bf16)


def transform(table, rows):
    return pl.pallas_call(
        table_kernel,
        grid=(3,),
        in_specs=[pl.BlockSpec((384, 1152), lambda t: (t, 0)), whole((1152, 384))],
        out_specs=pl.BlockSpec((384, 384), lambda t: (t, 0)),
        out_shape=struct((1152, 384), bf16),
        compiler_params=ROOM,
    )(table, rows)


def filter_kernel(
    rows, fwd, inv, mix_in, mix_out, bias_in, bias_out, back, low, first, active, second, total
):
    grid = mm(fwd[0], rows[...]).astype(bf16)
    grid = jnp.concatenate([grid[:288], grid[288:]], axis=1)
    low[...] = grid
    value = mm(grid, mix_in[...]) + bias_in[...]
    first[...] = value
    half, _ = gelu_parts(value)
    hot = (value * half).astype(bf16)
    active[...] = hot
    value = mm(hot, mix_out[...]) + bias_out[...]
    second[...] = value
    value = value - SHRINK * value * lax.rsqrt(value * value + SHRINK * SHRINK)
    value = value.astype(bf16)
    value = jnp.concatenate([value[:, :384], value[:, 384:]], axis=0)
    part = mm(inv[0], value)

    @pl.when(pl.program_id(0) == 0)
    def _():
        total[...] = part

    @pl.when(pl.program_id(0) == 1)
    def _():
        back[...] = (total[...] + part).astype(bf16)


def filter_forward(rows, fwd, inv, mix_in, mix_out, bias_in, bias_out):
    part = pl.BlockSpec((288, 768), lambda t: (t, 0))
    return pl.pallas_call(
        filter_kernel,
        grid=(2,),
        in_specs=[
            whole((1152, 384)),
            pl.BlockSpec((1, 576, 1152), lambda t: (t, 0, 0)),
            pl.BlockSpec((1, 1152, 576), lambda t: (t, 0, 0)),
            whole((768, 768)),
            whole((768, 768)),
            whole((1, 768)),
            whole((1, 768)),
        ],
        out_specs=[whole((1152, 384)), part, part, part, part],
        out_shape=[
            struct((1152, 384), bf16),
            struct((576, 768), bf16),
            struct((576, 768), f32),
            struct((576, 768), bf16),
            struct((576, 768), f32),
        ],
        scratch_shapes=[pltpu.VMEM((1152, 384), f32)],
        compiler_params=ROOM,
    )(rows, fwd, inv, mix_in, mix_out, bias_in, bias_out)


def filter_back_kernel(
    rows, inv_t, fwd_t, mix_in, mix_out, first, second, back, first_low, second_low, sums, total
):
    step = pl.program_id(0)
    grad = mm(inv_t[0], rows[...])
    grad = jnp.concatenate([grad[:288], grad[288:]], axis=1)
    value = second[...]
    root = lax.rsqrt(value * value + SHRINK * SHRINK)
    grad = grad * (1.0 - SHRINK * SHRINK * SHRINK * root * root * root)
    out_sum = jnp.sum(grad, axis=0, keepdims=True)
    grad = grad.astype(bf16)
    second_low[...] = grad
    value = first[...]
    half, bell = gelu_parts(value)
    grad = outer_cols(grad, mix_out[...]) * (half + value * bell)
    in_sum = jnp.sum(grad, axis=0, keepdims=True)
    grad = grad.astype(bf16)
    first_low[...] = grad
    grad = outer_cols(grad, mix_in[...]).astype(bf16)
    grad = jnp.concatenate([grad[:, :384], grad[:, 384:]], axis=0)
    part = mm(fwd_t[0], grad)

    @pl.when(step == 0)
    def _():
        total[...] = part
        sums[0:1, :] = in_sum
        sums[1:2, :] = out_sum

    @pl.when(step == 1)
    def _():
        back[...] = (total[...] + part).astype(bf16)
        sums[0:1, :] += in_sum
        sums[1:2, :] += out_sum


def filter_backward(rows, inv_t, fwd_t, mix_in, mix_out, first, second):
    part = pl.BlockSpec((288, 768), lambda t: (t, 0))
    return pl.pallas_call(
        filter_back_kernel,
        grid=(2,),
        in_specs=[
            whole((1152, 384)),
            pl.BlockSpec((1, 576, 1152), lambda t: (t, 0, 0)),
            pl.BlockSpec((1, 1152, 576), lambda t: (t, 0, 0)),
            whole((768, 768)),
            whole((768, 768)),
            part,
            part,
        ],
        out_specs=[whole((1152, 384)), part, part, whole((2, 768))],
        out_shape=[
            struct((1152, 384), bf16),
            struct((576, 768), bf16),
            struct((576, 768), bf16),
            struct((2, 768), f32),
        ],
        scratch_shapes=[pltpu.VMEM((1152, 384), f32)],
        compiler_params=ROOM,
    )(rows, inv_t, fwd_t, mix_in, mix_out, first, second)


def filter_grads_kernel(low, first_low, active, second_low, mask, fold, out):
    for which, (left, right) in enumerate(((low, first_low), (active, second_low))):
        grad = inner_rows(left[...], right[...])
        real = grad[:384, :384] + grad[384:, 384:]
        imag = grad[:384, 384:] - grad[384:, :384]
        for part, value in enumerate((real, imag)):
            blocks = mm((value * mask[...]).astype(bf16), fold[...]).astype(bf16)
            for piece in range(3):
                at = which * 768 + part * 384 + piece * 128
                group, row = at // 256, at % 256
                out[row : row + 128, group * 128 : group * 128 + 128] = blocks[
                    piece * 128 : piece * 128 + 128
                ]


def filter_grads(low, first_low, active, second_low, mask, fold):
    return pl.pallas_call(
        filter_grads_kernel,
        out_shape=struct((256, 768), bf16),
        compiler_params=ROOM,
    )(low, first_low, active, second_low, mask, fold)


def chain_kernel(
    x, present, filtered, cotangent, gain_first, shift_first, gain, shift, w_in, w_out, units,
    stream, mixed, grad_low, hidden, grad_pre, grad_stream, packed, sums, unit_sums,
    rows, normed, scale, total,
):
    step = pl.program_id(0)

    @pl.when(step == 0)
    def _():
        rows[...] = jnp.zeros_like(rows)
        total[...] = jnp.zeros_like(total)
        sums[...] = jnp.zeros_like(sums)
        for s in range(4):
            here = slice(144 * s, 144 * s + 144)
            there = present[here]
            value = widen(rows, x.at[s])
            first, _ = standard(value)
            masked = (first * gain_first[...] + shift_first[...]) * there
            value = value + both_halves(filtered, s) + masked
            stream[here] = value
            value, spread_of = standard(value.astype(bf16).astype(f32))
            normed[here] = value
            scale[here] = spread_of
            mixed[here] = (value * gain[...] + shift[...]).astype(bf16)
            value = widen(rows, cotangent.at[s]) * there
            sums[2:3, :] += jnp.sum(value, axis=0, keepdims=True)
            grad_low[here] = value.astype(bf16)

    into = w_in[...].reshape(768, 768)
    outof = w_out[...].reshape(768, 768)
    unit_total = jnp.zeros((1, 768), f32)
    for b in range(2):
        here = slice(288 * b, 288 * b + 288)
        value = mm(mixed[here], into) + units[0]
        half, bell = gelu_parts(value)
        hidden[0, here] = (value * half).astype(bf16)
        grad = outer_cols(grad_low[here], outof) * (half + value * bell)
        unit_total += jnp.sum(grad, axis=0, keepdims=True)
        grad = grad.astype(bf16)
        grad_pre[0, here] = grad
        total[here] += outer_cols(grad, into).astype(bf16).astype(f32)
    unit_sums[0] = unit_total

    @pl.when(step == 3)
    def _():
        for s in range(4):
            here = slice(144 * s, 144 * s + 144)
            grad = total[here]
            value = normed[here]
            sums[0:1, :] += jnp.sum(grad * value, axis=0, keepdims=True)
            sums[1:2, :] += jnp.sum(grad, axis=0, keepdims=True)
            grad = grad * gain[...]
            grad = grad - jnp.mean(grad, axis=-1, keepdims=True) - value * jnp.mean(
                grad * value, axis=-1, keepdims=True
            )
            grad = widen(rows, cotangent.at[s]) + scale[here] * grad
            grad_stream[here] = grad
            packed[0, s] = grad[:, :384].astype(bf16)
            packed[1, s] = grad[:, 384:].astype(bf16)


def chain(x, present, filtered, cotangent, gain_first, shift_first, gain, shift, weights, units):
    group = pl.BlockSpec((1, 576, 768), lambda g: (g, 0, 0))
    return pl.pallas_call(
        chain_kernel,
        grid=(4,),
        in_specs=[
            whole((4, 3, LON, 768)),
            whole((576, 1)),
            whole((2, 4, 144, 384)),
            whole((4, 3, LON, 768)),
            whole((1, 768)),
            whole((1, 768)),
            whole((1, 768)),
            whole((1, 768)),
            pl.BlockSpec((16, 1, PAD, 768), lambda g: (0, g, 0, 0)),
            pl.BlockSpec((16, 1, PAD, 768), lambda g: (1, g, 0, 0)),
            pl.BlockSpec((1, 1, 768), lambda g: (g, 0, 0)),
        ],
        out_specs=[
            whole((576, 768)),
            whole((576, 768)),
            whole((576, 768)),
            group,
            group,
            whole((576, 768)),
            whole((2, 4, 144, 384)),
            whole((3, 768)),
            pl.BlockSpec((1, 1, 768), lambda g: (g, 0, 0)),
        ],
        out_shape=[
            struct((576, 768), f32),
            struct((576, 768), bf16),
            struct((576, 768), bf16),
            struct((4, 576, 768), bf16),
            struct((4, 576, 768), bf16),
            struct((576, 768), f32),
            struct((2, 4, 144, 384), bf16),
            struct((3, 768), f32),
            struct((4, 1, 768), f32),
        ],
        scratch_shapes=[
            pltpu.VMEM((144, 768), f32),
            pltpu.VMEM((576, 768), f32),
            pltpu.VMEM((576, 1), f32),
            pltpu.VMEM((576, 768), f32),
        ],
        compiler_params=ROOM,
    )(x, present, filtered, cotangent, gain_first, shift_first, gain, shift, weights, weights, units)


def weight_grads_kernel(core, mixed, grad_pre, hidden, grad_low, out):
    @pl.when(pl.program_id(1) == 0)
    def _():
        out[...] = inner_rows(mixed[...], grad_pre[0]).astype(bf16).reshape(1, 16, 1, PAD, 768)

    @pl.when(pl.program_id(1) == 1)
    def _():
        out[...] = inner_rows(hidden[0], grad_low[...]).astype(bf16).reshape(1, 16, 1, PAD, 768)


def weight_grads(core, mixed, grad_pre, hidden, grad_low):
    group = pl.BlockSpec((1, 576, 768), lambda g, w, c: (g, 0, 0))
    return pl.pallas_call(
        weight_grads_kernel,
        grid_spec=pltpu.PrefetchScalarGridSpec(
            num_scalar_prefetch=1,
            grid=(4, 2),
            in_specs=[whole((576, 768)), group, group, whole((576, 768))],
            out_specs=pl.BlockSpec(
                (1, 16, 1, PAD, 768), lambda g, w, c: ((w + c[0]) % 2, 0, g, 0, 0)
            ),
        ),
        out_shape=struct((2, 16, 4, PAD, 768), bf16),
        compiler_params=ROOM,
    )(core, mixed, grad_pre, hidden, grad_low)


def output_kernel(hidden, w_out, stream, present, bias, out, total):
    step = pl.program_id(0)
    part = mm(hidden[0], w_out[...].reshape(768, 768)).astype(bf16).astype(f32)

    @pl.when(step == 0)
    def _():
        total[...] = part

    @pl.when(step > 0)
    def _():
        total[...] += part

    @pl.when(step == 3)
    def _():
        for s in range(4):
            here = slice(144 * s, 144 * s + 144)
            value = stream[here] + present[here] * (total[here] + bias[...])
            for i in range(3):
                out[s, i] = value[PAD * i : PAD * i + LON].astype(bf16)


def layer_output(hidden, weights, stream, present, bias):
    return pl.pallas_call(
        output_kernel,
        grid=(4,),
        in_specs=[
            pl.BlockSpec((1, 576, 768), lambda g: (g, 0, 0)),
            pl.BlockSpec((16, 1, PAD, 768), lambda g: (1, g, 0, 0)),
            whole((576, 768)),
            whole((576, 1)),
            whole((1, 768)),
        ],
        out_specs=whole((4, 3, LON, 768)),
        out_shape=struct((4, 3, LON, 768), bf16),
        scratch_shapes=[pltpu.VMEM((576, 768), f32)],
        compiler_params=ROOM,
    )(hidden, weights, stream, present, bias)


def final_kernel(x, present, from_spec, grad_stream, gain, out, sums, rows):
    @pl.when(pl.program_id(0) == 0)
    def _():
        sums[...] = jnp.zeros_like(sums)

    rows[...] = jnp.zeros_like(rows)
    normed, scale = standard(widen(rows, x.at[0]))
    stream = grad_stream[...]
    grad = (both_halves(from_spec, 0) + stream) * present[...]
    sums[0:1, :] += jnp.sum(grad * normed, axis=0, keepdims=True)
    sums[1:2, :] += jnp.sum(grad, axis=0, keepdims=True)
    grad = grad * gain[...]
    grad = grad - jnp.mean(grad, axis=-1, keepdims=True) - normed * jnp.mean(
        grad * normed, axis=-1, keepdims=True
    )
    grad = stream + scale * grad
    for i in range(3):
        out[0, i] = grad[PAD * i : PAD * i + LON]


def input_grads(x, present, from_spec, grad_stream, gain):
    return pl.pallas_call(
        final_kernel,
        grid=(4,),
        in_specs=[
            pl.BlockSpec((1, 3, LON, 768), lambda s: (s, 0, 0, 0)),
            pl.BlockSpec((144, 1), lambda s: (s, 0)),
            pl.BlockSpec((2, 1, 144, 384), lambda s: (0, s, 0, 0)),
            pl.BlockSpec((144, 768), lambda s: (s, 0)),
            whole((1, 768)),
        ],
        out_specs=[
            pl.BlockSpec((1, 3, LON, 768), lambda s: (s, 0, 0, 0)),
            whole((2, 768)),
        ],
        out_shape=[struct((4, 3, LON, 768), f32), struct((2, 768), f32)],
        scratch_shapes=[pltpu.VMEM((144, 768), f32)],
        compiler_params=ROOM,
    )(x, present, from_spec, grad_stream, gain)


def swap(value, axes):
    return lax.all_to_all(value, axes, 0, 0, tiled=True)


def spread(value, axes, count):
    return swap(jnp.broadcast_to(value[None], (count,) + value.shape), axes)


def shifted(value, by):
    return lax.ppermute(value, "mlp", [(i, (i + by) % 4) for i in range(4)])


def across(rows):
    return swap(rows.reshape(16, 72, 384), XY).reshape(1152, 384)


def narrow(rows):
    return jnp.concatenate([rows[..., :384], rows[..., 384:]], axis=-2)


def broad(rows):
    n = rows.shape[-2] // 2
    return jnp.concatenate([rows[..., :n, :], rows[..., n:, :]], axis=-1)


def block_form(weights):
    eye = jnp.eye(4, dtype=weights.dtype)
    dense = jnp.einsum("pbef,bc->pbecf", weights, eye).reshape(2, 384, 384)
    return jnp.concatenate(
        [
            jnp.concatenate([dense[0], dense[1]], axis=1),
            jnp.concatenate([-dense[1], dense[0]], axis=1),
        ],
        axis=0,
    )


def total_of(vector):
    near = jnp.sum(spread(vector, ("dp", "core", "mlp"), 16), axis=0)
    return jnp.sum(spread(near, XY, 16), axis=0)


def after(value, *others):
    return lax.optimization_barrier((value,) + others)[0]


def shards(
    inputs,
    validity,
    gain_first,
    shift_first,
    spectral_in,
    spectral_in_bias,
    spectral_out,
    spectral_out_bias,
    gain_second,
    shift_second,
    weight_in,
    bias_in,
    weight_out,
    bias_out,
    cotangent,
):
    core = lax.axis_index("core")
    group = lax.axis_index("mlp")
    table = {name: jnp.asarray(value) for name, value in tables().items()}
    mask, fold = (jnp.asarray(value) for value in block_fold())
    gain_first, shift_first, gain_second, shift_second, bias_out = (
        value.reshape(1, 768)
        for value in (gain_first, shift_first, gain_second, shift_second, bias_out)
    )

    wide = lax.axis_index(("x", "y", "core"))
    both = jnp.concatenate([weight_in, weight_out], axis=0)
    piece = lax.dynamic_slice_in_dim(both, wide * PAD, PAD, 0)
    piece = jnp.stack([piece] + [shifted(piece, d) for d in (1, 2, 3)])
    weights = lax.all_gather(piece, ("x", "y", "core"))

    present = jnp.pad(validity.astype(f32), ((0, 0), (0, 0), (0, PAD - LON))).reshape(576, 1)
    packed = norm_pack(inputs, present, gain_first, shift_first)
    tokens = swap(packed.reshape(8, 144, 384), PAIR)

    small = after(
        jnp.concatenate([bias_in, spectral_in_bias.reshape(-1), spectral_out_bias.reshape(-1)]), tokens
    )
    filters = after(jnp.stack([spectral_in, spectral_out]), tokens)
    small = jnp.stack([small] + [shifted(small, d) for d in (1, 2, 3)])
    filters = jnp.stack([filters] + [shifted(filters, d) for d in (1, 2, 3)])

    def my_half(value):
        pair = [
            lax.dynamic_index_in_dim(value, (group - 2 * core - u) % 4, 0, keepdims=False)
            for u in range(2)
        ]
        return jnp.concatenate(pair, axis=1)

    units = small[:, :768].reshape(4, 1, 768)
    mix_in = block_form(my_half(filters[:, 0]))
    mix_out = block_form(my_half(filters[:, 1]))
    mix_in_bias = my_half(small[:, 768:1152].reshape(4, 2, 2, 96)).reshape(1, 768)
    mix_out_bias = my_half(small[:, 1152:].reshape(4, 2, 2, 96)).reshape(1, 768)

    spectrum = transform(table["lon_fwd"], tokens.reshape(1152, 384))
    back, grid_low, first, active, second = filter_forward(
        across(spectrum),
        table["grid_fwd"],
        table["grid_inv"],
        mix_in,
        mix_out,
        mix_in_bias,
        mix_out_bias,
    )
    filtered = transform(table["lon_inv"], across(back))
    filtered = swap(filtered.reshape(8, 144, 384), PAIR).reshape(2, 4, 144, 384)

    stream, mixed, grad_low, hidden, grad_pre, grad_stream, packed, sums, unit_sums = chain(
        inputs,
        present,
        filtered,
        cotangent,
        gain_first,
        shift_first,
        gain_second,
        shift_second,
        weights,
        units,
    )
    tokens = swap(packed.reshape(8, 144, 384), PAIR)
    slots = weight_grads(core.astype(jnp.int32).reshape(1), mixed, grad_pre, hidden, grad_low)
    taken = lax.ppermute(slots[1], "core", [(0, 1), (1, 0)])
    share = (slots[0].astype(f32) + taken.astype(f32)).astype(bf16).reshape(3072, 768)
    share = lax.psum_scatter(share, "x", scatter_dimension=0, tiled=True)
    share = lax.psum_scatter(share, "y", scatter_dimension=0, tiled=True)
    output = layer_output(hidden, weights, stream, present, bias_out)

    grad_columns = across(transform(table["lon_inv_t"], tokens.reshape(1152, 384)))
    grad_spectrum, first_low, second_low, filter_sums = filter_backward(
        grad_columns, table["grid_inv_t"], table["grid_fwd_t"], mix_in, mix_out, first, second
    )
    filter_share = filter_grads(grid_low, first_low, active, second_low, mask, fold)
    joined = swap(
        jnp.concatenate(
            [grad_spectrum.reshape(16, 72, 384), narrow(filter_share.reshape(16, 16, 768))], axis=1
        ),
        XY,
    )
    grad_rows = joined[:, :72].reshape(1152, 384)
    filter_share = jnp.sum(joined[:, 72:].astype(f32), axis=0).astype(bf16)
    from_spec = transform(table["lon_fwd_t"], grad_rows)

    order = (group - jnp.arange(4, dtype=jnp.int32)) % 4
    share = jnp.take(narrow(share.reshape(4, PAD, 768)), order, axis=0)
    share = jnp.broadcast_to(share[None], (2, 4, 96, 384)).reshape(8, 96, 384)
    joined = swap(
        jnp.concatenate(
            [
                from_spec.reshape(8, 144, 384),
                share,
                jnp.broadcast_to(filter_share[None], (8, 32, 384)),
            ],
            axis=1,
        ),
        PAIR,
    )
    from_spec = joined[:, :144].reshape(2, 4, 144, 384)
    share = jnp.sum(joined[:, 144:].reshape(2, 4, 128, 384).astype(f32), axis=1).astype(bf16)
    other = lax.ppermute(share, "dp", [(0, 1), (1, 0)])
    share = (share.astype(f32) + other.astype(f32)).astype(bf16)
    gathered = lax.all_gather(share, XY)
    grad_slices = broad(gathered[:, :, :96]).swapaxes(0, 1).reshape(2, 768, 768).astype(f32)
    filters = broad(gathered[:, :, 96:]).reshape(16, 2, 16, 6, 128)[..., :96]
    filters = filters.transpose(1, 3, 0, 2, 4).reshape(2, 2, 2, 4, 96, 96)
    filters = filters.transpose(1, 2, 0, 3, 4, 5).reshape(2, 2, 8, 96, 96).astype(f32)

    grad_inputs, first_sums = input_grads(inputs, present, from_spec, grad_stream, gain_first)

    filter_sums = filter_sums.reshape(2, 2, 1, 384)
    filter_sums = jnp.where(
        core == jnp.arange(2, dtype=jnp.int32)[None, None, :, None], filter_sums, 0.0
    )
    unit_sums = jnp.take(unit_sums.reshape(4, 768), order, axis=0)
    small = total_of(
        jnp.concatenate(
            [first_sums, sums, unit_sums, filter_sums.reshape(4, 768), jnp.zeros((3, 768), f32)]
        )
    )
    filter_sums = small[9:13].reshape(2, 2, 8, 96)
    unit_sums = lax.dynamic_index_in_dim(small[5:9], group, 0, keepdims=False)

    def mine(vector):
        return lax.dynamic_slice_in_dim(vector, group * 192, 192, 0)

    return (
        output,
        grad_inputs,
        mine(small[0]),
        mine(small[1]),
        filters[0],
        filter_sums[0],
        filters[1],
        filter_sums[1],
        mine(small[2]),
        mine(small[3]),
        grad_slices[0],
        unit_sums,
        grad_slices[1],
        mine(small[4]),
    )


def solution(mesh):
    fine = Mesh(mesh.devices.reshape(2, 4, 4, 2, 4), EVERY)
    tokens = P("dp", ("x", "y", "core"), "mlp")
    placed = (
        tokens,
        tokens,
        P(),
        P(),
        P(None, "mlp"),
        P(None, "mlp"),
        P(None, "mlp"),
        P(None, "mlp"),
        P(),
        P(),
        P(None, "mlp"),
        P("mlp"),
        P("mlp", None),
        P(),
        tokens,
    )
    return jax.shard_map(
        shards,
        mesh=fine,
        in_specs=placed,
        out_specs=(
            tokens,
            tokens,
            P("mlp"),
            P("mlp"),
            P(),
            P(),
            P(),
            P(),
            P("mlp"),
            P("mlp"),
            P(None, "mlp"),
            P("mlp"),
            P("mlp", None),
            P("mlp"),
        ),
        check_vma=False,
    )
```

```python
import math

import jax
import jax.numpy as jnp
import numpy as np
from jax import lax
from jax.experimental import pallas as pl
from jax.experimental.pallas import tpu as pltpu
from jax.sharding import Mesh
from jax.sharding import PartitionSpec as P

H = 96
KWP = 96
W = 180
LON = 45
PAD = 48
EPSILON = 1e-05
SHRINK = 0.01
ROOT_HALF = math.sqrt(0.5)
ROOT_TWO_PI = math.sqrt(2.0 * math.pi)

XY = ("x", "y")
PAIR = ("core", "mlp")
EVERY = ("dp", "x", "y", "core", "mlp")
bf16 = jnp.bfloat16
f32 = jnp.float32
ROOM = pltpu.CompilerParams(vmem_limit_bytes=50 * 1024 * 1024)


def tables():
    w = np.arange(W)
    k = np.arange(KWP)
    phase = 2.0 * np.pi * ((w[:, None] * k[None, :]) % W) / W
    live = np.where(k < W // 2 + 1, 1.0 / math.sqrt(W), 0.0)
    weight = np.where((k == 0) | (2 * k == W), 1.0, 2.0) * live
    fwd = np.stack([np.cos(phase) * live, -np.sin(phase) * live], axis=2)
    inv = np.stack([np.cos(phase) * weight, -np.sin(phase) * weight], axis=2)
    pad = ((0, 0), (0, PAD - LON), (0, 0), (0, 0))
    fwd = np.pad(fwd.reshape(4, LON, KWP, 2), pad).reshape(4, PAD, 16, 6, 2)
    inv = np.pad(inv.reshape(4, LON, KWP, 2), pad).reshape(4, PAD, 16, 6, 2)
    same = np.eye(6).reshape(2, 3, 6)
    lon_fwd = np.einsum("mwqkp,rih->qhkprmiw", fwd, same).reshape(1152, 1152)
    lon_inv = np.einsum("mwqkp,rih->rmiwqhkp", inv, same).reshape(1152, 1152)
    h = np.arange(H)
    angle = 2.0 * np.pi * ((h[:, None] * h[None, :]) % H) / H
    cos = np.cos(angle) / math.sqrt(H)
    sin = np.sin(angle) / math.sqrt(H)
    lat_fwd = np.stack([np.stack([cos, sin]), np.stack([-sin, cos])])
    lat_inv = np.stack([np.stack([cos, -sin]), np.stack([sin, cos])])
    kk = np.eye(6).reshape(2, 3, 6)
    grid_fwd = np.einsum("pqjah,tkl->tpkjahlq", lat_fwd.reshape(2, 2, H, 16, 6), kk)
    grid_inv = np.einsum("pqahj,tkl->tahlpqkj", lat_inv.reshape(2, 2, 16, 6, H), kk)
    grid_fwd = grid_fwd.reshape(2, 576, 1152)
    grid_inv = grid_inv.reshape(2, 1152, 576)

    def low(table):
        return np.ascontiguousarray(table).astype(np.float32).astype(bf16)

    return {
        "lon_fwd": low(lon_fwd),
        "lon_inv": low(lon_inv),
        "lon_fwd_t": low(lon_fwd.T),
        "lon_inv_t": low(lon_inv.T),
        "grid_fwd": low(grid_fwd),
        "grid_inv": low(grid_inv),
        "grid_fwd_t": low(grid_fwd.swapaxes(1, 2)),
        "grid_inv_t": low(grid_inv.swapaxes(1, 2)),
    }


def block_fold():
    at = np.arange(384) // 96
    mask = (at[:, None] == at[None, :]).astype(np.float32)
    fold = np.tile(np.eye(96, 128), (4, 1)).astype(np.float32)
    return mask.astype(bf16), fold.astype(bf16)


def mm(left, right):
    return jnp.dot(left, right, preferred_element_type=f32)


def inner_rows(left, right):
    return lax.dot_general(left, right, (((0,), (0,)), ((), ())), preferred_element_type=f32)


def outer_cols(left, right):
    return lax.dot_general(left, right, (((1,), (1,)), ((), ())), preferred_element_type=f32)


def gelu_parts(value):
    half = 0.5 * (1.0 + lax.erf(value * ROOT_HALF))
    return half, jnp.exp(-0.5 * value * value) * (1.0 / ROOT_TWO_PI)


def standard(value):
    centred = value - jnp.mean(value, axis=-1, keepdims=True)
    scale = lax.rsqrt(jnp.mean(centred * centred, axis=-1, keepdims=True) + EPSILON)
    return centred * scale, scale


def widen(rows, source):
    for i in range(3):
        rows[PAD * i : PAD * i + LON, :] = source[i].astype(f32)
    return rows[...]


def whole(shape):
    return pl.BlockSpec(shape, lambda *_: (0,) * len(shape))


def struct(shape, dtype):
    return jax.ShapeDtypeStruct(shape, dtype)


def pack(first, second, m):
    here = slice(192 * m, 192 * m + 192)
    return jnp.concatenate([first[:, here], second[:, here]], axis=1)


def unpack(pieces, r, s2):
    here = slice(192 * s2, 192 * s2 + 192)
    return jnp.concatenate([pieces[r, m][:, here] for m in range(4)], axis=1).astype(f32)


def norm_kernel(x, present, gain, shift, out, rows):
    rows[...] = jnp.zeros_like(rows)
    pair = []
    for s2 in range(2):
        normed, _ = standard(widen(rows, x.at[s2]))
        here = slice(144 * s2, 144 * s2 + 144)
        pair.append(((normed * gain[...] + shift[...]) * present[here]).astype(bf16))
    for m in range(4):
        out[0, m] = pack(pair[0], pair[1], m)


def norm_pack(inputs, present, gain, shift):
    return pl.pallas_call(
        norm_kernel,
        grid=(2,),
        in_specs=[
            pl.BlockSpec((2, 3, LON, 768), lambda r: (r, 0, 0, 0)),
            pl.BlockSpec((288, 1), lambda r: (r, 0)),
            whole((1, 768)),
            whole((1, 768)),
        ],
        out_specs=pl.BlockSpec((1, 4, 144, 384), lambda r: (r, 0, 0, 0)),
        out_shape=struct((2, 4, 144, 384), bf16),
        scratch_shapes=[pltpu.VMEM((144, 768), f32)],
        compiler_params=ROOM,
    )(inputs, present, gain, shift)


def mix_kernel(w_in, w_out, mask, mix_in, mix_out):
    for source, out in ((w_in, mix_in), (w_out, mix_out)):
        parts = []
        for part in range(2):
            row = jnp.concatenate([source[part, 0], source[part, 1]], axis=1)
            row = jnp.concatenate([row, row], axis=1)
            parts.append(jnp.concatenate([row] * 4, axis=0) * mask[...])
        out[:384, :384] = parts[0]
        out[384:, 384:] = parts[0]
        out[:384, 384:] = parts[1]
        out[384:, :384] = -parts[1]


def mixers(w_in, w_out, mask):
    return pl.pallas_call(
        mix_kernel,
        out_shape=[struct((768, 768), bf16)] * 2,
        compiler_params=ROOM,
    )(w_in, w_out, mask)


def table_kernel(table, rows, out):
    out[...] = mm(table[...], rows[...]).astype(bf16)


def transform(table, rows):
    return pl.pallas_call(
        table_kernel,
        grid=(3,),
        in_specs=[pl.BlockSpec((384, 1152), lambda t: (t, 0)), whole((1152, 384))],
        out_specs=pl.BlockSpec((384, 384), lambda t: (t, 0)),
        out_shape=struct((1152, 384), bf16),
        compiler_params=ROOM,
    )(table, rows)


def filter_kernel(
    rows, fwd, inv, mix_in, mix_out, bias_in, bias_out, back, low, first, active, second, total
):
    grid = mm(fwd[0], rows[...]).astype(bf16)
    grid = jnp.concatenate([grid[:288], grid[288:]], axis=1)
    low[...] = grid
    value = mm(grid, mix_in[...]) + bias_in[...]
    first[...] = value
    half, _ = gelu_parts(value)
    hot = (value * half).astype(bf16)
    active[...] = hot
    value = mm(hot, mix_out[...]) + bias_out[...]
    second[...] = value
    value = value - SHRINK * value * lax.rsqrt(value * value + SHRINK * SHRINK)
    value = value.astype(bf16)
    value = jnp.concatenate([value[:, :384], value[:, 384:]], axis=0)
    part = mm(inv[0], value)

    @pl.when(pl.program_id(0) == 0)
    def _():
        total[...] = part

    @pl.when(pl.program_id(0) == 1)
    def _():
        back[...] = (total[...] + part).astype(bf16)


def filter_forward(rows, fwd, inv, mix_in, mix_out, bias_in, bias_out):
    part = pl.BlockSpec((288, 768), lambda t: (t, 0))
    return pl.pallas_call(
        filter_kernel,
        grid=(2,),
        in_specs=[
            whole((1152, 384)),
            pl.BlockSpec((1, 576, 1152), lambda t: (t, 0, 0)),
            pl.BlockSpec((1, 1152, 576), lambda t: (t, 0, 0)),
            whole((768, 768)),
            whole((768, 768)),
            whole((1, 768)),
            whole((1, 768)),
        ],
        out_specs=[whole((1152, 384)), part, part, part, part],
        out_shape=[
            struct((1152, 384), bf16),
            struct((576, 768), bf16),
            struct((576, 768), f32),
            struct((576, 768), bf16),
            struct((576, 768), f32),
        ],
        scratch_shapes=[pltpu.VMEM((1152, 384), f32)],
        compiler_params=ROOM,
    )(rows, fwd, inv, mix_in, mix_out, bias_in, bias_out)


def filter_back_kernel(
    rows, inv_t, fwd_t, mix_in, mix_out, first, second, back, first_low, second_low, sums, total
):
    step = pl.program_id(0)
    grad = mm(inv_t[0], rows[...])
    grad = jnp.concatenate([grad[:288], grad[288:]], axis=1)
    value = second[...]
    root = lax.rsqrt(value * value + SHRINK * SHRINK)
    grad = grad * (1.0 - SHRINK * SHRINK * SHRINK * root * root * root)
    out_sum = jnp.sum(grad, axis=0, keepdims=True)
    grad = grad.astype(bf16)
    second_low[...] = grad
    value = first[...]
    half, bell = gelu_parts(value)
    grad = outer_cols(grad, mix_out[...]) * (half + value * bell)
    in_sum = jnp.sum(grad, axis=0, keepdims=True)
    grad = grad.astype(bf16)
    first_low[...] = grad
    grad = outer_cols(grad, mix_in[...]).astype(bf16)
    grad = jnp.concatenate([grad[:, :384], grad[:, 384:]], axis=0)
    part = mm(fwd_t[0], grad)

    @pl.when(step == 0)
    def _():
        total[...] = part
        sums[0:1, :] = in_sum
        sums[1:2, :] = out_sum

    @pl.when(step == 1)
    def _():
        back[...] = (total[...] + part).astype(bf16)
        sums[0:1, :] += in_sum
        sums[1:2, :] += out_sum


def filter_backward(rows, inv_t, fwd_t, mix_in, mix_out, first, second):
    part = pl.BlockSpec((288, 768), lambda t: (t, 0))
    return pl.pallas_call(
        filter_back_kernel,
        grid=(2,),
        in_specs=[
            whole((1152, 384)),
            pl.BlockSpec((1, 576, 1152), lambda t: (t, 0, 0)),
            pl.BlockSpec((1, 1152, 576), lambda t: (t, 0, 0)),
            whole((768, 768)),
            whole((768, 768)),
            part,
            part,
        ],
        out_specs=[whole((1152, 384)), part, part, whole((2, 768))],
        out_shape=[
            struct((1152, 384), bf16),
            struct((576, 768), bf16),
            struct((576, 768), bf16),
            struct((2, 768), f32),
        ],
        scratch_shapes=[pltpu.VMEM((1152, 384), f32)],
        compiler_params=ROOM,
    )(rows, inv_t, fwd_t, mix_in, mix_out, first, second)


def filter_grads_kernel(low, first_low, active, second_low, mask, fold, out):
    for which, (left, right) in enumerate(((low, first_low), (active, second_low))):
        grad = inner_rows(left[...], right[...])
        real = grad[:384, :384] + grad[384:, 384:]
        imag = grad[:384, 384:] - grad[384:, :384]
        for part, value in enumerate((real, imag)):
            value = value * mask[...].astype(f32)
            blocks = mm((value[:192] + value[192:]).astype(bf16), fold[...]).astype(bf16)
            for piece in range(3):
                at = which * 384 + part * 192 + piece * 64
                group, row = at // 128, at % 128
                out[row : row + 64, group * 128 : group * 128 + 128] = blocks[
                    piece * 64 : piece * 64 + 64
                ]


def filter_grads(low, first_low, active, second_low, mask, fold):
    return pl.pallas_call(
        filter_grads_kernel,
        out_shape=struct((128, 768), bf16),
        compiler_params=ROOM,
    )(low, first_low, active, second_low, mask, fold)


def chain_kernel(
    x, present, filtered, cotangent, gain_first, shift_first, gain, shift, w_in, w_out, units,
    stream, mixed, grad_low, hidden, grad_pre, grad_stream, packed, sums, unit_sums,
    rows, normed, scale, total,
):
    step = pl.program_id(0)

    @pl.when(step == 0)
    def _():
        rows[...] = jnp.zeros_like(rows)
        total[...] = jnp.zeros_like(total)
        sums[...] = jnp.zeros_like(sums)
        for s in range(4):
            here = slice(144 * s, 144 * s + 144)
            there = present[here]
            value = widen(rows, x.at[s])
            first, _ = standard(value)
            masked = (first * gain_first[...] + shift_first[...]) * there
            value = value + unpack(filtered, s // 2, s % 2) + masked
            stream[here] = value
            value, spread_of = standard(value.astype(bf16).astype(f32))
            normed[here] = value
            scale[here] = spread_of
            mixed[here] = (value * gain[...] + shift[...]).astype(bf16)
            value = widen(rows, cotangent.at[s]) * there
            sums[2:3, :] += jnp.sum(value, axis=0, keepdims=True)
            grad_low[here] = value.astype(bf16)

    into = w_in[...].reshape(768, 768)
    outof = w_out[...].reshape(768, 768)
    unit_total = jnp.zeros((1, 768), f32)
    for b in range(2):
        here = slice(288 * b, 288 * b + 288)
        value = mm(mixed[here], into) + units[0]
        half, bell = gelu_parts(value)
        hidden[0, here] = (value * half).astype(bf16)
        grad = outer_cols(grad_low[here], outof) * (half + value * bell)
        unit_total += jnp.sum(grad, axis=0, keepdims=True)
        grad = grad.astype(bf16)
        grad_pre[0, here] = grad
        total[here] += outer_cols(grad, into).astype(bf16).astype(f32)
    unit_sums[0] = unit_total

    @pl.when(step == 3)
    def _():
        lows = []
        for s in range(4):
            here = slice(144 * s, 144 * s + 144)
            grad = total[here]
            value = normed[here]
            sums[0:1, :] += jnp.sum(grad * value, axis=0, keepdims=True)
            sums[1:2, :] += jnp.sum(grad, axis=0, keepdims=True)
            grad = grad * gain[...]
            grad = grad - jnp.mean(grad, axis=-1, keepdims=True) - value * jnp.mean(
                grad * value, axis=-1, keepdims=True
            )
            grad = widen(rows, cotangent.at[s]) + scale[here] * grad
            grad_stream[here] = grad
            lows.append(grad.astype(bf16))
        for r in range(2):
            for m in range(4):
                packed[r, m] = pack(lows[2 * r], lows[2 * r + 1], m)


def chain(x, present, filtered, cotangent, gain_first, shift_first, gain, shift, weights, units):
    group = pl.BlockSpec((1, 576, 768), lambda g: (g, 0, 0))
    return pl.pallas_call(
        chain_kernel,
        grid=(4,),
        in_specs=[
            whole((4, 3, LON, 768)),
            whole((576, 1)),
            whole((2, 4, 144, 384)),
            whole((4, 3, LON, 768)),
            whole((1, 768)),
            whole((1, 768)),
            whole((1, 768)),
            whole((1, 768)),
            pl.BlockSpec((16, 1, PAD, 768), lambda g: (0, g, 0, 0)),
            pl.BlockSpec((16, 1, PAD, 768), lambda g: (1, g, 0, 0)),
            pl.BlockSpec((1, 1, 768), lambda g: (g, 0, 0)),
        ],
        out_specs=[
            whole((576, 768)),
            whole((576, 768)),
            whole((576, 768)),
            group,
            group,
            whole((576, 768)),
            whole((2, 4, 144, 384)),
            whole((3, 768)),
            pl.BlockSpec((1, 1, 768), lambda g: (g, 0, 0)),
        ],
        out_shape=[
            struct((576, 768), f32),
            struct((576, 768), bf16),
            struct((576, 768), bf16),
            struct((4, 576, 768), bf16),
            struct((4, 576, 768), bf16),
            struct((576, 768), f32),
            struct((2, 4, 144, 384), bf16),
            struct((3, 768), f32),
            struct((4, 1, 768), f32),
        ],
        scratch_shapes=[
            pltpu.VMEM((144, 768), f32),
            pltpu.VMEM((576, 768), f32),
            pltpu.VMEM((576, 1), f32),
            pltpu.VMEM((576, 768), f32),
        ],
        compiler_params=ROOM,
    )(x, present, filtered, cotangent, gain_first, shift_first, gain, shift, weights, weights, units)


def weight_grads_kernel(mixed, grad_pre, hidden, grad_low, out):
    @pl.when(pl.program_id(1) == 0)
    def _():
        out[...] = inner_rows(mixed[...], grad_pre[0]).astype(bf16).reshape(16, 1, 1, PAD, 768)

    @pl.when(pl.program_id(1) == 1)
    def _():
        out[...] = inner_rows(hidden[0], grad_low[...]).astype(bf16).reshape(16, 1, 1, PAD, 768)


def weight_grads(mixed, grad_pre, hidden, grad_low):
    group = pl.BlockSpec((1, 576, 768), lambda g, w: (g, 0, 0))
    return pl.pallas_call(
        weight_grads_kernel,
        grid=(4, 2),
        in_specs=[whole((576, 768)), group, group, whole((576, 768))],
        out_specs=pl.BlockSpec((16, 1, 1, PAD, 768), lambda g, w: (0, w, g, 0, 0)),
        out_shape=struct((16, 2, 4, PAD, 768), bf16),
        compiler_params=ROOM,
    )(mixed, grad_pre, hidden, grad_low)


def output_kernel(hidden, w_out, stream, present, bias, out, total):
    step = pl.program_id(0)
    part = mm(hidden[0], w_out[...].reshape(768, 768)).astype(bf16).astype(f32)

    @pl.when(step == 0)
    def _():
        total[...] = part

    @pl.when(step > 0)
    def _():
        total[...] += part

    @pl.when(step == 3)
    def _():
        for s in range(4):
            here = slice(144 * s, 144 * s + 144)
            value = stream[here] + present[here] * (total[here] + bias[...])
            for i in range(3):
                out[s, i] = value[PAD * i : PAD * i + LON].astype(bf16)


def layer_output(hidden, weights, stream, present, bias):
    return pl.pallas_call(
        output_kernel,
        grid=(4,),
        in_specs=[
            pl.BlockSpec((1, 576, 768), lambda g: (g, 0, 0)),
            pl.BlockSpec((16, 1, PAD, 768), lambda g: (1, g, 0, 0)),
            whole((576, 768)),
            whole((576, 1)),
            whole((1, 768)),
        ],
        out_specs=whole((4, 3, LON, 768)),
        out_shape=struct((4, 3, LON, 768), bf16),
        scratch_shapes=[pltpu.VMEM((576, 768), f32)],
        compiler_params=ROOM,
    )(hidden, weights, stream, present, bias)


def final_kernel(x, present, from_spec, grad_stream, gain, out, sums, rows):
    @pl.when(pl.program_id(0) == 0)
    def _():
        sums[...] = jnp.zeros_like(sums)

    rows[...] = jnp.zeros_like(rows)
    for s2 in range(2):
        here = slice(144 * s2, 144 * s2 + 144)
        normed, scale = standard(widen(rows, x.at[s2]))
        stream = grad_stream[here]
        grad = (unpack(from_spec, 0, s2) + stream) * present[here]
        sums[0:1, :] += jnp.sum(grad * normed, axis=0, keepdims=True)
        sums[1:2, :] += jnp.sum(grad, axis=0, keepdims=True)
        grad = grad * gain[...]
        grad = grad - jnp.mean(grad, axis=-1, keepdims=True) - normed * jnp.mean(
            grad * normed, axis=-1, keepdims=True
        )
        grad = stream + scale * grad
        for i in range(3):
            out[s2, i] = grad[PAD * i : PAD * i + LON]


def input_grads(x, present, from_spec, grad_stream, gain):
    return pl.pallas_call(
        final_kernel,
        grid=(2,),
        in_specs=[
            pl.BlockSpec((2, 3, LON, 768), lambda r: (r, 0, 0, 0)),
            pl.BlockSpec((288, 1), lambda r: (r, 0)),
            pl.BlockSpec((1, 4, 144, 384), lambda r: (r, 0, 0, 0)),
            pl.BlockSpec((288, 768), lambda r: (r, 0)),
            whole((1, 768)),
        ],
        out_specs=[
            pl.BlockSpec((2, 3, LON, 768), lambda r: (r, 0, 0, 0)),
            whole((2, 768)),
        ],
        out_shape=[struct((4, 3, LON, 768), f32), struct((2, 768), f32)],
        scratch_shapes=[pltpu.VMEM((144, 768), f32)],
        compiler_params=ROOM,
    )(x, present, from_spec, grad_stream, gain)


def gather_kernel(rows, out):
    near = rows[...].astype(f32)
    near = near[0] + near[1]
    every = near[0] + near[1] + near[2] + near[3]
    small = jnp.concatenate(
        [every[56:65]] + [near[m, 65:66] for m in range(4)] + [jnp.zeros((3, 768), f32)], axis=0
    )
    value = jnp.concatenate(
        [every[:PAD]] + [near[m, PAD : PAD + 8] for m in range(4)] + [small], axis=0
    ).astype(bf16)
    for q in range(16):
        out[q] = value


def gather_rows(rows):
    return pl.pallas_call(
        gather_kernel,
        out_shape=struct((16, 96, 768), bf16),
        compiler_params=ROOM,
    )(rows)


def finish_kernel(place, own, other, w_in, w_out, f_in, f_out, small, units, biases):
    core, group = place[0], place[1]
    own_share = own[:, :PAD].reshape(768, 768).astype(f32)
    other_share = other[:, :PAD].reshape(768, 768).astype(f32)

    @pl.when(core == 0)
    def _():
        w_in[...] = own_share
        w_out[...] = other_share

    @pl.when(core == 1)
    def _():
        w_in[...] = other_share
        w_out[...] = own_share

    rest = own[:, PAD:].astype(f32) + other[:, PAD:].astype(f32)
    for m in range(4):
        rows = rest[:, 8 * m : 8 * m + 8].reshape(128, 768)
        for which, out in enumerate((f_in, f_out)):
            for part in range(2):
                for b in range(2):
                    pieces = []
                    for piece in range(3):
                        at = which * 384 + part * 192 + b * 96 + piece * 32
                        u, row = at // 128, at % 128
                        pieces.append(rows[row : row + 32, 128 * u : 128 * u + 128])
                    out[part, 2 * m + b] = jnp.concatenate(pieces, axis=0)[:, :96]
    sums = jnp.sum(rest[:, 32:], axis=0)
    small[...] = jnp.zeros_like(small)
    for k in range(4):

        @pl.when(group == k)
        def _():
            small[0:5, :] = sums[0:5, 192 * k : 192 * k + 192]
            units[...] = sums[5 + k : 6 + k]

    biases[...] = sums[9:13]


def finish(place, own, other):
    vmem = pl.BlockSpec(memory_space=pltpu.VMEM)
    return pl.pallas_call(
        finish_kernel,
        in_specs=[pl.BlockSpec(memory_space=pltpu.SMEM), vmem, vmem],
        out_specs=[vmem] * 7,
        out_shape=[
            struct((768, 768), f32),
            struct((768, 768), f32),
            struct((2, 8, 96, 96), f32),
            struct((2, 8, 96, 96), f32),
            struct((8, 192), f32),
            struct((1, 768), f32),
            struct((4, 768), f32),
        ],
        compiler_params=ROOM,
    )(place, own, other)


def swap(value, axes):
    return lax.all_to_all(value, axes, 0, 0, tiled=True)


def shifted(value, by):
    return lax.ppermute(value, "mlp", [(i, (i + by) % 4) for i in range(4)])


def across(rows):
    return swap(rows.reshape(16, 72, 384), XY).reshape(1152, 384)


def narrow(rows):
    return jnp.concatenate([rows[..., :384], rows[..., 384:]], axis=-2)


def after(value, *others):
    return lax.optimization_barrier((value,) + others)[0]


def shards(
    inputs,
    validity,
    gain_first,
    shift_first,
    spectral_in,
    spectral_in_bias,
    spectral_out,
    spectral_out_bias,
    gain_second,
    shift_second,
    weight_in,
    bias_in,
    weight_out,
    bias_out,
    cotangent,
):
    core = lax.axis_index("core")
    group = lax.axis_index("mlp")
    table = {name: jnp.asarray(value) for name, value in tables().items()}
    mask, fold = (jnp.asarray(value) for value in block_fold())
    gain_first, shift_first, gain_second, shift_second, bias_out = (
        value.reshape(1, 768)
        for value in (gain_first, shift_first, gain_second, shift_second, bias_out)
    )

    wide = lax.axis_index(("x", "y", "core"))
    high = lax.reduce_precision(bias_in, 8, 7)
    middle = lax.reduce_precision(bias_in - high, 8, 7)
    bias_rows = jnp.stack([high, middle, bias_in - high - middle]).astype(bf16)
    both = jnp.concatenate([weight_in, weight_out], axis=0)
    piece = jnp.concatenate(
        [
            lax.dynamic_slice_in_dim(both, wide * PAD, PAD, 0),
            bias_rows,
            jnp.zeros((13, 768), bf16),
        ]
    )
    pieces = jnp.stack([piece] + [shifted(piece, d) for d in (1, 2, 3)])

    present = jnp.pad(validity.astype(f32), ((0, 0), (0, 0), (0, PAD - LON))).reshape(576, 1)
    packed = norm_pack(inputs, present, gain_first, shift_first)
    tokens = swap(packed.reshape(8, 144, 384), PAIR)

    pieces = after(pieces, tokens)
    weights = lax.all_gather(pieces[:, :PAD], ("x", "y", "core"))
    units = pieces[:, PAD : PAD + 3].astype(f32)
    units = (units[:, 0] + units[:, 1] + units[:, 2]).reshape(4, 1, 768)

    mix_in, mix_out = mixers(spectral_in, spectral_out, mask)
    mix_in_bias, mix_out_bias = (
        jnp.tile(value.reshape(2, 1, 192), (1, 2, 1)).reshape(1, 768)
        for value in (spectral_in_bias, spectral_out_bias)
    )

    spectrum = transform(table["lon_fwd"], tokens.reshape(1152, 384))
    back, grid_low, first, active, second = filter_forward(
        across(spectrum),
        table["grid_fwd"],
        table["grid_inv"],
        mix_in,
        mix_out,
        mix_in_bias,
        mix_out_bias,
    )
    filtered = transform(table["lon_inv"], across(back))
    filtered = swap(filtered.reshape(8, 144, 384), PAIR).reshape(2, 4, 144, 384)

    stream, mixed, grad_low, hidden, grad_pre, grad_stream, packed, sums, unit_sums = chain(
        inputs,
        present,
        filtered,
        cotangent,
        gain_first,
        shift_first,
        gain_second,
        shift_second,
        weights,
        units,
    )
    share = weight_grads(mixed, grad_pre, hidden, grad_low).reshape(6144, 768)
    share = lax.psum_scatter(share, ("x", "y", "core"), scatter_dimension=0, tiled=True)
    tokens = swap(packed.reshape(8, 144, 384), PAIR)
    output = layer_output(hidden, weights, stream, present, bias_out)

    grad_columns = across(transform(table["lon_inv_t"], tokens.reshape(1152, 384)))
    grad_spectrum, first_low, second_low, filter_sums = filter_backward(
        grad_columns, table["grid_inv_t"], table["grid_fwd_t"], mix_in, mix_out, first, second
    )
    filter_share = filter_grads(grid_low, first_low, active, second_low, mask, fold)
    joined = swap(
        jnp.concatenate(
            [grad_spectrum.reshape(16, 72, 384), narrow(filter_share.reshape(16, 8, 768))], axis=1
        ),
        XY,
    )
    grad_rows = joined[:, :72].reshape(1152, 384)
    filter_share = jnp.sum(joined[:, 72:].astype(f32), axis=0).astype(bf16)
    filter_share = jnp.concatenate([filter_share[:8], filter_share[8:]], axis=1)
    from_spec = transform(table["lon_fwd_t"], grad_rows)
    from_spec = swap(from_spec.reshape(8, 144, 384), PAIR).reshape(2, 4, 144, 384)
    grad_inputs, first_sums = input_grads(inputs, present, from_spec, grad_stream, gain_first)

    order = (group - jnp.arange(4, dtype=jnp.int32)) % 4
    unit_sums = jnp.take(unit_sums.reshape(4, 768), order, axis=0)
    filter_sums = jnp.sum(filter_sums.reshape(2, 2, 2, 192), axis=2).reshape(1, 768)
    small = jnp.concatenate(
        [first_sums, sums, unit_sums, filter_sums, jnp.zeros((6, 768), f32)]
    ).astype(bf16)
    share = jnp.take(share.reshape(4, PAD, 768), order, axis=0)
    rest = jnp.concatenate([filter_share, small])
    rows = jnp.concatenate([share, jnp.broadcast_to(rest[None], (4, 24, 768))], axis=1)
    rows = jnp.broadcast_to(rows[None], (2, 4, 72, 768)).reshape(8, 72, 768)
    rows = swap(rows, ("dp", "mlp")).reshape(2, 4, 72, 768)
    rows = swap(gather_rows(rows), XY)
    other = lax.ppermute(rows, "core", [(0, 1), (1, 0)])
    grad_w_in, grad_w_out, grad_f_in, grad_f_out, small, unit_sums, biases = finish(
        jnp.stack([core, group]).astype(jnp.int32), rows, other
    )
    biases = biases.reshape(4, 2, 2, 2, 96).transpose(1, 2, 0, 3, 4).reshape(2, 2, 8, 96)
    return (
        output,
        grad_inputs,
        small[0],
        small[1],
        grad_f_in,
        biases[0],
        grad_f_out,
        biases[1],
        small[2],
        small[3],
        grad_w_in,
        unit_sums.reshape(768),
        grad_w_out,
        small[4],
    )


def solution(mesh):
    fine = Mesh(mesh.devices.reshape(2, 4, 4, 2, 4), EVERY)
    tokens = P("dp", ("x", "y", "core"), "mlp")
    placed = (
        tokens,
        tokens,
        P(),
        P(),
        P(None, "mlp"),
        P(None, "mlp"),
        P(None, "mlp"),
        P(None, "mlp"),
        P(),
        P(),
        P(None, "mlp"),
        P("mlp"),
        P("mlp", None),
        P(),
        tokens,
    )
    return jax.shard_map(
        shards,
        mesh=fine,
        in_specs=placed,
        out_specs=(
            tokens,
            tokens,
            P("mlp"),
            P("mlp"),
            P(),
            P(),
            P(),
            P(),
            P("mlp"),
            P("mlp"),
            P(None, "mlp"),
            P("mlp"),
            P("mlp", None),
            P("mlp"),
        ),
        check_vma=False,
    )
```

```python
import math

import jax
import jax.numpy as jnp
import numpy as np
from jax import lax
from jax.experimental import pallas as pl
from jax.experimental.pallas import tpu as pltpu
from jax.sharding import Mesh
from jax.sharding import PartitionSpec as P

H = 96
KWP = 96
W = 180
LON = 45
PAD = 48
EPSILON = 1e-05
SHRINK = 0.01
ROOT_HALF = math.sqrt(0.5)
ROOT_TWO_PI = math.sqrt(2.0 * math.pi)

XY = ("x", "y")
WIDE = ("x", "y", "core")
EVERY = ("dp", "x", "y", "core", "mlp")
bf16 = jnp.bfloat16
f32 = jnp.float32
ROOM = pltpu.CompilerParams(vmem_limit_bytes=50 * 1024 * 1024)


def tables():
    w = np.arange(W)
    k = np.arange(KWP)
    phase = 2.0 * np.pi * ((w[:, None] * k[None, :]) % W) / W
    live = np.where(k < W // 2 + 1, 1.0 / math.sqrt(W), 0.0)
    weight = np.where((k == 0) | (2 * k == W), 1.0, 2.0) * live
    fwd = np.stack([np.cos(phase) * live, -np.sin(phase) * live], axis=2)
    inv = np.stack([np.cos(phase) * weight, -np.sin(phase) * weight], axis=2)
    pad = ((0, 0), (0, PAD - LON), (0, 0), (0, 0))
    fwd = np.pad(fwd.reshape(4, LON, KWP, 2), pad).reshape(4, PAD, 32, 3, 2)
    inv = np.pad(inv.reshape(4, LON, KWP, 2), pad).reshape(4, PAD, 32, 3, 2)
    eye = np.eye(3)

    def columns(table):
        table = table.reshape(32, 18, -1)
        return np.pad(table, ((0, 0), (0, 6), (0, 0))).reshape(768, -1)

    lon_fwd = columns(np.einsum("mwvkp,ia->vakpmiw", fwd, eye))
    lon_inv = columns(np.einsum("mwvkp,ia->vakpmiw", inv, eye))
    h = np.arange(H)
    angle = 2.0 * np.pi * ((h[:, None] * h[None, :]) % H) / H
    cos = np.cos(angle) / math.sqrt(H)
    sin = np.sin(angle) / math.sqrt(H)
    lat_fwd = np.stack([np.stack([cos, sin]), np.stack([-sin, cos])])
    lat_inv = np.stack([np.stack([cos, -sin]), np.stack([sin, cos])])
    grid_fwd = columns(np.einsum("pqjva,kl->valqpkj", lat_fwd.reshape(2, 2, H, 32, 3), eye))
    grid_inv = columns(np.einsum("pqvaj,kl->valpqkj", lat_inv.reshape(2, 2, 32, 3, H), eye))

    def low(table):
        return np.ascontiguousarray(table).astype(np.float32).astype(bf16)

    return {
        "lon_fwd": low(lon_fwd),
        "lon_inv": low(lon_inv.T),
        "lon_fwd_t": low(lon_fwd.T),
        "lon_inv_t": low(lon_inv),
        "grid_fwd": low(grid_fwd.T),
        "grid_inv": low(grid_inv),
        "grid_fwd_t": low(grid_fwd),
        "grid_inv_t": low(grid_inv.T),
        "place": low(np.pad(np.eye(128).reshape(32, 4, 128), ((0, 0), (18, 2), (0, 0))).reshape(768, 128)),
    }


def block_fold():
    at = np.arange(384) // 96
    mask = (at[:, None] == at[None, :]).astype(np.float32)
    fold = np.tile(np.eye(96, 128), (4, 1)).astype(np.float32)
    return mask.astype(bf16), fold.astype(bf16)


def mm(left, right):
    return jnp.dot(left, right, preferred_element_type=f32)


def inner_rows(left, right):
    return lax.dot_general(left, right, (((0,), (0,)), ((), ())), preferred_element_type=f32)


def outer_cols(left, right):
    return lax.dot_general(left, right, (((1,), (1,)), ((), ())), preferred_element_type=f32)


def gelu_parts(value):
    half = 0.5 * (1.0 + lax.erf(value * ROOT_HALF))
    return half, jnp.exp(-0.5 * value * value) * (1.0 / ROOT_TWO_PI)


def standard(value):
    centred = value - jnp.mean(value, axis=-1, keepdims=True)
    scale = lax.rsqrt(jnp.mean(centred * centred, axis=-1, keepdims=True) + EPSILON)
    return centred * scale, scale


def widen(rows, source):
    for i in range(3):
        rows[PAD * i : PAD * i + LON, :] = source[i].astype(f32)
    return rows[...]


def cost(us):
    return pl.CostEstimate(flops=us * 1100000000, bytes_accessed=us * 1000000, transcendentals=0)


def whole(shape):
    return pl.BlockSpec(shape, lambda *_: (0,) * len(shape))


def struct(shape, dtype):
    return jax.ShapeDtypeStruct(shape, dtype)


PIECES = [struct((144, 768), bf16)] * 4
GROUPS = pltpu.VMEM((4, 144, 768), bf16)
SMEM = pl.BlockSpec(memory_space=pltpu.SMEM)
VMEM = pl.BlockSpec(memory_space=pltpu.VMEM)


def pack(values, by_group):
    for m in range(4):
        here = slice(192 * m, 192 * m + 192)
        by_group[m] = jnp.concatenate([value[:, here] for value in values], axis=1)


def unpack(by_group, s):
    here = slice(192 * s, 192 * s + 192)
    return jnp.concatenate([by_group[m][:, here] for m in range(4)], axis=1).astype(f32)


def send(group, by_group, *outs):
    for d in range(4):
        outs[d][...] = by_group[(group + d) % 4]


def receive(group, first, second, third, fourth, by_group):
    for d, piece in enumerate((first, second, third, fourth)):
        by_group[(group + 4 - d) % 4] = piece[...]


def shifted(value, by):
    return lax.ppermute(value, "mlp", [(i, (i + by) % 4) for i in range(4)])


def exchange(*pieces):
    return [pieces[0]] + [shifted(pieces[d], d) for d in (1, 2, 3)]


RECEIVED = [(144, 768)] * 4


def norm_kernel(group, x, present, gain, shift, first, second, third, fourth, rows, by_group):
    rows[...] = jnp.zeros_like(rows)
    values = []
    for s in range(4):
        normed, _ = standard(widen(rows, x.at[s]))
        masked = (normed * gain[...] + shift[...]) * present[144 * s : 144 * s + 144]
        values.append(masked.astype(bf16))
    pack(values, by_group)
    send(group[0], by_group, first, second, third, fourth)


def norm_pack(group, inputs, present, gain, shift):
    return pl.pallas_call(
        norm_kernel,
        in_specs=[SMEM] + [VMEM] * 4,
        out_shape=PIECES,
        scratch_shapes=[pltpu.VMEM((144, 768), f32), GROUPS],
        cost_estimate=cost(10),
        compiler_params=ROOM,
    )(group, inputs, present, gain, shift)


def columns_kernel(group, table, first, second, third, fourth, out, by_group):
    receive(group[0], first, second, third, fourth, by_group)
    out[...] = mm(table[...], by_group[...].reshape(576, 768)).astype(bf16)


def to_columns(group, table, pieces):
    return pl.pallas_call(
        columns_kernel,
        in_specs=[SMEM] + [VMEM] * 5,
        out_shape=struct((768, 768), bf16),
        scratch_shapes=[GROUPS],
        cost_estimate=cost(2),
        compiler_params=ROOM,
    )(group, table, *pieces)


def pieces_kernel(group, table, columns, first, second, third, fourth, by_group):
    by_group[...] = mm(table[...], columns[...]).astype(bf16).reshape(4, 144, 768)
    send(group[0], by_group, first, second, third, fourth)


def to_pieces(group, table, columns):
    return pl.pallas_call(
        pieces_kernel,
        in_specs=[SMEM] + [VMEM] * 2,
        out_shape=PIECES,
        scratch_shapes=[GROUPS],
        cost_estimate=cost(2),
        compiler_params=ROOM,
    )(group, table, columns)


def mix_kernel(w_in, w_out, mask, mix_in, mix_out):
    for source, out in ((w_in, mix_in), (w_out, mix_out)):
        parts = []
        for part in range(2):
            row = jnp.concatenate([source[part, 0], source[part, 1]], axis=1)
            row = jnp.concatenate([row, row], axis=1)
            parts.append(jnp.concatenate([row] * 4, axis=0) * mask[...])
        out[:384, :384] = parts[0]
        out[384:, 384:] = parts[0]
        out[:384, 384:] = parts[1]
        out[384:, :384] = -parts[1]


def mixers(w_in, w_out, mask):
    return pl.pallas_call(
        mix_kernel,
        out_shape=[struct((768, 768), bf16)] * 2,
        cost_estimate=cost(1),
        compiler_params=ROOM,
    )(w_in, w_out, mask)


def table_kernel(table, rows, out):
    out[...] = mm(table[...], rows[...]).astype(bf16)


def transform(table, rows):
    return pl.pallas_call(
        table_kernel,
        grid=(3,),
        in_specs=[pl.BlockSpec((384, 1152), lambda t: (t, 0)), whole((1152, 384))],
        out_specs=pl.BlockSpec((384, 384), lambda t: (t, 0)),
        out_shape=struct((1152, 384), bf16),
        compiler_params=ROOM,
    )(table, rows)


def turn(value):
    return jnp.concatenate(
        [
            jnp.concatenate([value[:288, at : at + 384], value[288:, at : at + 384]], axis=1)
            for at in (0, 384)
        ],
        axis=0,
    )


def filter_kernel(
    columns, fwd, inv, mix_in, mix_out, bias_in, bias_out, back, low, first, active, second
):
    grid = turn(mm(fwd[...], columns[...]).astype(bf16))
    low[...] = grid
    value = mm(grid, mix_in[...]) + bias_in[...]
    first[...] = value
    half, _ = gelu_parts(value)
    hot = (value * half).astype(bf16)
    active[...] = hot
    value = mm(hot, mix_out[...]) + bias_out[...]
    second[...] = value
    value = value - SHRINK * value * lax.rsqrt(value * value + SHRINK * SHRINK)
    back[...] = mm(inv[...], turn(value.astype(bf16))).astype(bf16)


def filter_forward(columns, fwd, inv, mix_in, mix_out, bias_in, bias_out):
    return pl.pallas_call(
        filter_kernel,
        out_shape=[
            struct((768, 768), bf16),
            struct((576, 768), bf16),
            struct((576, 768), f32),
            struct((576, 768), bf16),
            struct((576, 768), f32),
        ],
        cost_estimate=cost(150),
        compiler_params=ROOM,
    )(columns, fwd, inv, mix_in, mix_out, bias_in, bias_out)


def filter_back_kernel(
    columns, inv_t, fwd_t, mix_in, mix_out, low, first, active, second, mask, fold, place,
    back, sums, share,
):
    grad = turn(mm(inv_t[...], columns[...]))
    value = second[...]
    root = lax.rsqrt(value * value + SHRINK * SHRINK)
    grad = grad * (1.0 - SHRINK * SHRINK * SHRINK * root * root * root)
    sums[1:2, :] = jnp.sum(grad, axis=0, keepdims=True)
    second_low = grad.astype(bf16)
    value = first[...]
    half, bell = gelu_parts(value)
    grad = outer_cols(second_low, mix_out[...]) * (half + value * bell)
    sums[0:1, :] = jnp.sum(grad, axis=0, keepdims=True)
    first_low = grad.astype(bf16)
    for which, (left, right) in enumerate(((low, first_low), (active, second_low))):
        grad = inner_rows(left[...], right)
        real = grad[:384, :384] + grad[384:, 384:]
        imag = grad[:384, 384:] - grad[384:, :384]
        for part, value in enumerate((real, imag)):
            value = value * mask[...].astype(f32)
            blocks = mm((value[:192] + value[192:]).astype(bf16), fold[...]).astype(bf16)
            for piece in range(3):
                at = which * 384 + part * 192 + piece * 64
                group, row = at // 128, at % 128
                share[row : row + 64, group * 128 : group * 128 + 128] = blocks[
                    piece * 64 : piece * 64 + 64
                ]
    grad = turn(outer_cols(first_low, mix_in[...]).astype(bf16))
    back[...] = (mm(fwd_t[...], grad) + mm(place[...], share[...])).astype(bf16)


def filter_backward(*operands):
    return pl.pallas_call(
        filter_back_kernel,
        out_shape=[struct((768, 768), bf16), struct((2, 768), f32)],
        scratch_shapes=[pltpu.VMEM((128, 768), bf16)],
        cost_estimate=cost(60),
        compiler_params=ROOM,
    )(*operands)


def prepare_kernel(x, present, cotangent, gain, shift, w_out, base, grad_low, back, sums, rows):
    @pl.when(pl.program_id(0) == 0)
    def _():
        rows[...] = jnp.zeros_like(rows)
        bias_sum = jnp.zeros((1, 768), f32)
        for s in range(4):
            here = slice(144 * s, 144 * s + 144)
            there = present[here]
            value = widen(rows, x.at[s])
            normed, _ = standard(value)
            base[here] = value + (normed * gain[...] + shift[...]) * there
            value = widen(rows, cotangent.at[s]) * there
            bias_sum += jnp.sum(value, axis=0, keepdims=True)
            grad_low[here] = value.astype(bf16)
        sums[...] = bias_sum

    back[0] = outer_cols(grad_low[...], w_out[...].reshape(768, 768))


def prepare(x, present, cotangent, gain, shift, weights):
    return pl.pallas_call(
        prepare_kernel,
        grid=(4,),
        in_specs=[
            whole((4, 3, LON, 768)),
            whole((576, 1)),
            whole((4, 3, LON, 768)),
            whole((1, 768)),
            whole((1, 768)),
            pl.BlockSpec((16, 1, PAD, 768), lambda g: (1, g, 0, 0)),
        ],
        out_specs=[
            whole((576, 768)),
            whole((576, 768)),
            pl.BlockSpec((1, 576, 768), lambda g: (g, 0, 0)),
            whole((1, 768)),
        ],
        out_shape=[
            struct((576, 768), f32),
            struct((576, 768), bf16),
            struct((4, 576, 768), f32),
            struct((1, 768), f32),
        ],
        scratch_shapes=[pltpu.VMEM((144, 768), f32)],
        compiler_params=ROOM,
        cost_estimate=cost(6),
    )(x, present, cotangent, gain, shift, weights)


def chain_kernel(
    at, base, in1, in2, in3, in4, cotangent, gain, shift, w_in, back, units,
    stream, mixed, hidden, grad_pre, grad_stream, out1, out2, out3, out4, sums, unit_sums,
    rows, normed, scale, total, by_group,
):
    step = pl.program_id(0)

    @pl.when(step == 0)
    def _():
        rows[...] = jnp.zeros_like(rows)
        total[...] = jnp.zeros_like(total)
        receive(at[0], in1, in2, in3, in4, by_group)
        for s in range(4):
            here = slice(144 * s, 144 * s + 144)
            value = base[here] + unpack(by_group, s)
            stream[here] = value
            value, spread_of = standard(value.astype(bf16).astype(f32))
            normed[here] = value
            scale[here] = spread_of
            mixed[here] = (value * gain[...] + shift[...]).astype(bf16)

    into = w_in[...].reshape(768, 768)
    value = mm(mixed[...], into) + units[0]
    half, bell = gelu_parts(value)
    hidden[0] = (value * half).astype(bf16)
    grad = back[0] * (half + value * bell)
    unit_sums[0] = jnp.sum(grad, axis=0, keepdims=True)
    grad = grad.astype(bf16)
    grad_pre[0] = grad
    total[...] += outer_cols(grad, into).astype(bf16).astype(f32)

    @pl.when(step == 3)
    def _():
        lows = []
        norm_sum = jnp.zeros((1, 768), f32)
        plain_sum = jnp.zeros((1, 768), f32)
        for s in range(4):
            here = slice(144 * s, 144 * s + 144)
            grad = total[here]
            value = normed[here]
            norm_sum += jnp.sum(grad * value, axis=0, keepdims=True)
            plain_sum += jnp.sum(grad, axis=0, keepdims=True)
            grad = grad * gain[...]
            grad = grad - jnp.mean(grad, axis=-1, keepdims=True) - value * jnp.mean(
                grad * value, axis=-1, keepdims=True
            )
            grad = widen(rows, cotangent.at[s]) + scale[here] * grad
            grad_stream[here] = grad
            lows.append(grad.astype(bf16))
        sums[0:1, :] = norm_sum
        sums[1:2, :] = plain_sum
        pack(lows, by_group)
        send(at[0], by_group, out1, out2, out3, out4)


def chain(group, base, pieces, cotangent, gain, shift, weights, back, units):
    by_step = pl.BlockSpec((1, 576, 768), lambda g: (g, 0, 0))
    outs = pl.pallas_call(
        chain_kernel,
        grid=(4,),
        in_specs=[
            SMEM,
            whole((576, 768)),
            *[whole(shape) for shape in RECEIVED],
            whole((4, 3, LON, 768)),
            whole((1, 768)),
            whole((1, 768)),
            pl.BlockSpec((16, 1, PAD, 768), lambda g: (0, g, 0, 0)),
            by_step,
            pl.BlockSpec((1, 1, 768), lambda g: (g, 0, 0)),
        ],
        out_specs=[
            *[whole((576, 768))] * 2,
            by_step,
            by_step,
            whole((576, 768)),
            *[whole(piece.shape) for piece in PIECES],
            whole((2, 768)),
            pl.BlockSpec((1, 1, 768), lambda g: (g, 0, 0)),
        ],
        out_shape=[
            struct((576, 768), f32),
            struct((576, 768), bf16),
            struct((4, 576, 768), bf16),
            struct((4, 576, 768), bf16),
            struct((576, 768), f32),
            *PIECES,
            struct((2, 768), f32),
            struct((4, 1, 768), f32),
        ],
        scratch_shapes=[
            pltpu.VMEM((144, 768), f32),
            pltpu.VMEM((576, 768), f32),
            pltpu.VMEM((576, 1), f32),
            pltpu.VMEM((576, 768), f32),
            GROUPS,
        ],
        compiler_params=ROOM,
        cost_estimate=cost(14),
    )(group, base, *pieces, cotangent, gain, shift, weights, back, units)
    return outs[:5], outs[5:9], outs[9], outs[10]


def share_kernel(core, mixed, grad_pre, hidden, grad_low, *rest):
    own = len(rest) == 2
    out = rest[-1]

    def store(value):
        value = value.reshape(16, 1, PAD, 768)
        if own:
            value = value + rest[0][...].astype(f32)
        out[...] = value.astype(bf16)

    @pl.when(core[0] == (0 if own else 1))
    def _():
        store(inner_rows(mixed[...], grad_pre[0]))

    @pl.when(core[0] == (1 if own else 0))
    def _():
        store(inner_rows(hidden[0], grad_low[...]))


def weight_share(core, mixed, grad_pre, hidden, grad_low, *given):
    by_step = pl.BlockSpec((1, 576, 768), lambda g: (g, 0, 0))
    pieces = pl.BlockSpec((16, 1, PAD, 768), lambda g: (0, g, 0, 0))
    return pl.pallas_call(
        share_kernel,
        grid=(4,),
        in_specs=[SMEM, whole((576, 768)), by_step, by_step, whole((576, 768))] + [pieces] * len(given),
        out_specs=pieces,
        out_shape=struct((16, 4, PAD, 768), bf16),
        compiler_params=ROOM,
        cost_estimate=cost(7),
    )(core, mixed, grad_pre, hidden, grad_low, *given)


def output_kernel(hidden, w_out, stream, present, bias, out, total):
    step = pl.program_id(0)
    part = mm(hidden[0], w_out[...].reshape(768, 768)).astype(bf16).astype(f32)

    @pl.when(step == 0)
    def _():
        total[...] = part

    @pl.when(step > 0)
    def _():
        total[...] += part

    @pl.when(step == 3)
    def _():
        for s in range(4):
            here = slice(144 * s, 144 * s + 144)
            value = stream[here] + present[here] * (total[here] + bias[...])
            for i in range(3):
                out[s, i] = value[PAD * i : PAD * i + LON].astype(bf16)


def layer_output(hidden, weights, stream, present, bias):
    return pl.pallas_call(
        output_kernel,
        grid=(4,),
        in_specs=[
            pl.BlockSpec((1, 576, 768), lambda g: (g, 0, 0)),
            pl.BlockSpec((16, 1, PAD, 768), lambda g: (1, g, 0, 0)),
            whole((576, 768)),
            whole((576, 1)),
            whole((1, 768)),
        ],
        out_specs=whole((4, 3, LON, 768)),
        out_shape=struct((4, 3, LON, 768), bf16),
        scratch_shapes=[pltpu.VMEM((576, 768), f32)],
        cost_estimate=cost(10),
        compiler_params=ROOM,
    )(hidden, weights, stream, present, bias)


def final_kernel(
    group, x, present, grad_stream, gain, first, second, third, fourth, out, sums, rows, by_group
):
    rows[...] = jnp.zeros_like(rows)
    receive(group[0], first, second, third, fourth, by_group)
    norm_sum = jnp.zeros((1, 768), f32)
    plain_sum = jnp.zeros((1, 768), f32)
    for s in range(4):
        here = slice(144 * s, 144 * s + 144)
        normed, scale = standard(widen(rows, x.at[s]))
        stream = grad_stream[here]
        grad = (unpack(by_group, s) + stream) * present[here]
        norm_sum += jnp.sum(grad * normed, axis=0, keepdims=True)
        plain_sum += jnp.sum(grad, axis=0, keepdims=True)
        grad = grad * gain[...]
        grad = grad - jnp.mean(grad, axis=-1, keepdims=True) - normed * jnp.mean(
            grad * normed, axis=-1, keepdims=True
        )
        grad = stream + scale * grad
        for i in range(3):
            out[s, i] = grad[PAD * i : PAD * i + LON]
    sums[0:1, :] = norm_sum
    sums[1:2, :] = plain_sum


def input_grads(group, x, present, grad_stream, gain, pieces):
    return pl.pallas_call(
        final_kernel,
        in_specs=[SMEM] + [VMEM] * 8,
        out_shape=[struct((4, 3, LON, 768), f32), struct((2, 768), f32)],
        scratch_shapes=[pltpu.VMEM((144, 768), f32), GROUPS],
        cost_estimate=cost(3),
        compiler_params=ROOM,
    )(group, x, present, grad_stream, gain, *pieces)


def gather_kernel(rows, out):
    near = rows[...].astype(f32)
    near = near[0] + near[1]
    every = near[0] + near[1] + near[2] + near[3]
    value = jnp.concatenate(
        [every[:PAD]]
        + [near[m, PAD : PAD + 4] for m in range(4)]
        + [every[52:61]]
        + [near[m, 61:62] for m in range(4)]
        + [jnp.zeros((3, 768), f32)],
        axis=0,
    ).astype(bf16)
    for q in range(16):
        out[q] = value


def gather_rows(rows):
    return pl.pallas_call(
        gather_kernel,
        out_shape=struct((16, 80, 768), bf16),
        cost_estimate=cost(2),
        compiler_params=ROOM,
    )(rows)


def finish_kernel(at, own, other, w_in, w_out, f_in, f_out, small, units, biases, joined):
    core, group = at[0], at[1]
    own_share = own[:, :PAD].reshape(768, 768).astype(f32)
    other_share = other[:, :PAD].reshape(768, 768).astype(f32)
    own_rest = own[:, PAD:].astype(f32)
    other_rest = other[:, PAD:].astype(f32)

    for k, (zero, one) in enumerate(((own_rest, other_rest), (other_rest, own_rest))):

        @pl.when(core == k)
        def _():
            (w_in, w_out)[k][...] = own_share
            (w_in, w_out)[1 - k][...] = other_share
            for m in range(4):
                joined[m, :, :4] = zero[:, 4 * m : 4 * m + 4]
                joined[m, :, 4:] = one[:, 4 * m : 4 * m + 4]

    for m in range(4):
        rows = joined[m].reshape(128, 768)
        for which, out in enumerate((f_in, f_out)):
            for part in range(2):
                for b in range(2):
                    pieces = []
                    for piece in range(3):
                        row = which * 384 + part * 192 + b * 96 + piece * 32
                        u, row = row // 128, row % 128
                        pieces.append(rows[row : row + 32, 128 * u : 128 * u + 128])
                    out[part, 2 * m + b] = jnp.concatenate(pieces, axis=0)[:, :96]
    sums = jnp.sum(own_rest[:, 16:] + other_rest[:, 16:], axis=0)
    small[...] = jnp.zeros_like(small)
    for k in range(4):

        @pl.when(group == k)
        def _():
            small[0:5, :] = sums[0:5, 192 * k : 192 * k + 192]
            units[...] = sums[5 + k : 6 + k]

    biases[...] = sums[9:13]


def finish(at, own, other):
    return pl.pallas_call(
        finish_kernel,
        in_specs=[SMEM, VMEM, VMEM],
        out_shape=[
            struct((768, 768), f32),
            struct((768, 768), f32),
            struct((2, 8, 96, 96), f32),
            struct((2, 8, 96, 96), f32),
            struct((8, 192), f32),
            struct((1, 768), f32),
            struct((4, 768), f32),
        ],
        scratch_shapes=[pltpu.VMEM((4, 16, 8, 768), f32)],
        cost_estimate=cost(5),
        compiler_params=ROOM,
    )(at, own, other)


def swap(value, axes):
    return lax.all_to_all(value, axes, 0, 0, tiled=True)


def across(columns):
    return swap(columns.reshape(32, 24, 768), WIDE).reshape(768, 768)


def after(value, *others):
    return lax.optimization_barrier((value,) + others)[0]


def shards(
    inputs,
    validity,
    gain_first,
    shift_first,
    spectral_in,
    spectral_in_bias,
    spectral_out,
    spectral_out_bias,
    gain_second,
    shift_second,
    weight_in,
    bias_in,
    weight_out,
    bias_out,
    cotangent,
):
    core = lax.axis_index("core")
    group = lax.axis_index("mlp")
    table = {name: jnp.asarray(value) for name, value in tables().items()}
    mask, fold = (jnp.asarray(value) for value in block_fold())
    gain_first, shift_first, gain_second, shift_second, bias_out = (
        value.reshape(1, 768)
        for value in (gain_first, shift_first, gain_second, shift_second, bias_out)
    )

    present = jnp.pad(validity.astype(f32), ((0, 0), (0, 0), (0, PAD - LON))).reshape(576, 1)
    here = group.astype(jnp.int32).reshape(1)
    sent_first = norm_pack(here, inputs, present, gain_first, shift_first)
    tokens = exchange(*sent_first)

    wide = lax.axis_index(WIDE)
    high = lax.reduce_precision(bias_in, 8, 7)
    middle = lax.reduce_precision(bias_in - high, 8, 7)
    bias_rows = jnp.stack([high, middle, bias_in - high - middle]).astype(bf16)
    both = jnp.concatenate([weight_in, weight_out], axis=0)
    piece = jnp.concatenate(
        [
            lax.dynamic_slice_in_dim(both, wide * PAD, PAD, 0),
            bias_rows,
            jnp.zeros((13, 768), bf16),
        ]
    )
    pieces = jnp.stack([piece] + [shifted(piece, d) for d in (1, 2, 3)])
    weights = lax.all_gather(pieces[:, :PAD], WIDE)
    units = pieces[:, PAD : PAD + 3].astype(f32)
    units = (units[:, 0] + units[:, 1] + units[:, 2]).reshape(4, 1, 768)

    mix_in, mix_out = mixers(spectral_in, spectral_out, mask)
    mix_in_bias, mix_out_bias = (
        jnp.tile(value.reshape(2, 1, 192), (1, 2, 1)).reshape(1, 768)
        for value in (spectral_in_bias, spectral_out_bias)
    )

    columns = across(to_columns(here, table["lon_fwd"], tokens))
    back, low, first, active, second = filter_forward(
        columns, table["grid_fwd"], table["grid_inv"], mix_in, mix_out, mix_in_bias, mix_out_bias
    )
    filtered = exchange(*to_pieces(here, table["lon_inv"], across(back)))
    base, grad_low, grad_hidden, bias_sum = prepare(
        inputs, present, cotangent, gain_first, shift_first, weights
    )
    (stream, mixed, hidden, grad_pre, grad_stream), sent, sums, unit_sums = chain(
        here, base, filtered, cotangent, gain_second, shift_second, weights, grad_hidden, units
    )
    operands = (core.astype(jnp.int32).reshape(1), mixed, grad_pre, hidden, grad_low)
    share = weight_share(*operands)
    share = weight_share(*operands, lax.ppermute(share, "core", [(0, 1), (1, 0)]))
    output = layer_output(hidden, weights, after(stream, share), present, bias_out)
    share = lax.psum_scatter(share.reshape(3072, 768), XY, scatter_dimension=0, tiled=True)

    columns = after(across(to_columns(here, table["lon_inv_t"], exchange(*sent))), output)
    back, filter_sums = filter_backward(
        columns,
        table["grid_inv_t"],
        table["grid_fwd_t"],
        mix_in,
        mix_out,
        low,
        first,
        active,
        second,
        mask,
        fold,
        table["place"],
    )
    back = across(back)
    filter_share = jnp.sum(back.reshape(32, 24, 768)[:, 18:22].astype(f32), axis=0).astype(bf16)
    from_spec = exchange(*to_pieces(here, table["lon_fwd_t"], back))
    grad_inputs, first_sums = input_grads(here, inputs, present, grad_stream, gain_first, from_spec)

    order = (group - jnp.arange(4, dtype=jnp.int32)) % 4
    unit_sums = jnp.take(unit_sums.reshape(4, 768), order, axis=0)
    filter_sums = jnp.sum(filter_sums.reshape(2, 2, 2, 192), axis=2).reshape(1, 768)
    rest = jnp.concatenate([first_sums, sums, bias_sum, unit_sums, filter_sums, jnp.zeros((2, 768), f32)])
    rest = jnp.concatenate([filter_share, rest.astype(bf16)])
    share = jnp.take(share.reshape(4, PAD, 768), order, axis=0)
    rows = jnp.concatenate([share, jnp.broadcast_to(rest[None], (4, 16, 768))], axis=1)
    rows = jnp.broadcast_to(rows[None], (2, 4, 64, 768)).reshape(8, 64, 768)
    rows = swap(rows, ("dp", "mlp")).reshape(2, 4, 64, 768)
    rows = swap(gather_rows(rows), XY)
    other = lax.ppermute(rows, "core", [(0, 1), (1, 0)])
    grad_w_in, grad_w_out, grad_f_in, grad_f_out, small, unit_sums, biases = finish(
        jnp.stack([core, group]).astype(jnp.int32), rows, other
    )
    biases = biases.reshape(4, 2, 2, 2, 96).transpose(1, 2, 0, 3, 4).reshape(2, 2, 8, 96)
    return (
        output,
        grad_inputs,
        small[0],
        small[1],
        grad_f_in,
        biases[0],
        grad_f_out,
        biases[1],
        small[2],
        small[3],
        grad_w_in,
        unit_sums.reshape(768),
        grad_w_out,
        small[4],
    )


def solution(mesh):
    fine = Mesh(mesh.devices.reshape(2, 4, 4, 2, 4), EVERY)
    tokens = P("dp", ("x", "y", "core"), "mlp")
    placed = (
        tokens,
        tokens,
        P(),
        P(),
        P(None, "mlp"),
        P(None, "mlp"),
        P(None, "mlp"),
        P(None, "mlp"),
        P(),
        P(),
        P(None, "mlp"),
        P("mlp"),
        P("mlp", None),
        P(),
        tokens,
    )
    return jax.shard_map(
        shards,
        mesh=fine,
        in_specs=placed,
        out_specs=(
            tokens,
            tokens,
            P("mlp"),
            P("mlp"),
            P(),
            P(),
            P(),
            P(),
            P("mlp"),
            P("mlp"),
            P(None, "mlp"),
            P("mlp"),
            P("mlp", None),
            P("mlp"),
        ),
        check_vma=False,
    )
```

```python
import math

import jax
import jax.numpy as jnp
import numpy as np
from jax import lax
from jax.experimental import pallas as pl
from jax.experimental.pallas import tpu as pltpu
from jax.sharding import Mesh
from jax.sharding import PartitionSpec as P

H = 96
KWP = 96
W = 180
LON = 45
PAD = 48
EPSILON = 1e-05
SHRINK = 0.01
ROOT_HALF = math.sqrt(0.5)
ROOT_TWO_PI = math.sqrt(2.0 * math.pi)

XY = ("x", "y")
WIDE = ("x", "y", "core")
EVERY = ("dp", "x", "y", "core", "mlp")
bf16 = jnp.bfloat16
f32 = jnp.float32
ROOM = pltpu.CompilerParams(vmem_limit_bytes=50 * 1024 * 1024)


def tables():
    w = np.arange(W)
    k = np.arange(KWP)
    phase = 2.0 * np.pi * ((w[:, None] * k[None, :]) % W) / W
    live = np.where(k < W // 2 + 1, 1.0 / math.sqrt(W), 0.0)
    weight = np.where((k == 0) | (2 * k == W), 1.0, 2.0) * live
    fwd = np.stack([np.cos(phase) * live, -np.sin(phase) * live], axis=2)
    inv = np.stack([np.cos(phase) * weight, -np.sin(phase) * weight], axis=2)
    pad = ((0, 0), (0, PAD - LON), (0, 0), (0, 0))
    fwd = np.pad(fwd.reshape(4, LON, KWP, 2), pad).reshape(4, PAD, 32, 3, 2)
    inv = np.pad(inv.reshape(4, LON, KWP, 2), pad).reshape(4, PAD, 32, 3, 2)
    eye = np.eye(3)

    def columns(table):
        table = table.reshape(32, 18, -1)
        return np.pad(table, ((0, 0), (0, 6), (0, 0))).reshape(768, -1)

    lon_fwd = columns(np.einsum("mwvkp,ia->vakpmiw", fwd, eye))
    lon_inv = columns(np.einsum("mwvkp,ia->vakpmiw", inv, eye))
    h = np.arange(H)
    angle = 2.0 * np.pi * ((h[:, None] * h[None, :]) % H) / H
    cos = np.cos(angle) / math.sqrt(H)
    sin = np.sin(angle) / math.sqrt(H)
    lat_fwd = np.stack([np.stack([cos, sin]), np.stack([-sin, cos])])
    lat_inv = np.stack([np.stack([cos, -sin]), np.stack([sin, cos])])
    grid_fwd = columns(np.einsum("pqjva,kl->valqpkj", lat_fwd.reshape(2, 2, H, 32, 3), eye))
    grid_inv = columns(np.einsum("pqvaj,kl->valpqkj", lat_inv.reshape(2, 2, 32, 3, H), eye))

    def low(table):
        return np.ascontiguousarray(table).astype(np.float32).astype(bf16)

    return {
        "lon_fwd": low(lon_fwd),
        "lon_inv": low(lon_inv.T),
        "lon_fwd_t": low(lon_fwd.T),
        "lon_inv_t": low(lon_inv),
        "grid_fwd": low(grid_fwd.T),
        "grid_inv": low(grid_inv),
        "grid_fwd_t": low(grid_fwd),
        "grid_inv_t": low(grid_inv.T),
        "place": low(np.pad(np.eye(128).reshape(32, 4, 128), ((0, 0), (18, 2), (0, 0))).reshape(768, 128)),
    }


def block_fold():
    at = np.arange(384) // 96
    mask = (at[:, None] == at[None, :]).astype(np.float32)
    fold = np.tile(np.eye(96, 128), (4, 1)).astype(np.float32)
    return mask.astype(bf16), fold.astype(bf16)


def mm(left, right):
    return jnp.dot(left, right, preferred_element_type=f32)


def inner_rows(left, right):
    return lax.dot_general(left, right, (((0,), (0,)), ((), ())), preferred_element_type=f32)


def outer_cols(left, right):
    return lax.dot_general(left, right, (((1,), (1,)), ((), ())), preferred_element_type=f32)


def gelu_parts(value):
    half = 0.5 * (1.0 + lax.erf(value * ROOT_HALF))
    return half, jnp.exp(-0.5 * value * value) * (1.0 / ROOT_TWO_PI)


def standard(value):
    centred = value - jnp.mean(value, axis=-1, keepdims=True)
    scale = lax.rsqrt(jnp.mean(centred * centred, axis=-1, keepdims=True) + EPSILON)
    return centred * scale, scale


def widen(rows, source):
    for i in range(3):
        rows[PAD * i : PAD * i + LON, :] = source[i].astype(f32)
    return rows[...]


def cost(us):
    return pl.CostEstimate(flops=us * 1100000000, bytes_accessed=us * 1000000, transcendentals=0)


def whole(shape):
    return pl.BlockSpec(shape, lambda *_: (0,) * len(shape))


def struct(shape, dtype):
    return jax.ShapeDtypeStruct(shape, dtype)


PIECES = [struct((144, 768), bf16)] * 4
GROUPS = pltpu.VMEM((4, 144, 768), bf16)
SMEM = pl.BlockSpec(memory_space=pltpu.SMEM)
VMEM = pl.BlockSpec(memory_space=pltpu.VMEM)


def pack(values, by_group):
    for m in range(4):
        here = slice(192 * m, 192 * m + 192)
        by_group[m] = jnp.concatenate([value[:, here] for value in values], axis=1)


def unpack(by_group, s):
    here = slice(192 * s, 192 * s + 192)
    return jnp.concatenate([by_group[m][:, here] for m in range(4)], axis=1).astype(f32)


def send(group, by_group, *outs):
    for d in range(4):
        outs[d][...] = by_group[(group + d) % 4]


def receive(group, first, second, third, fourth, by_group):
    for d, piece in enumerate((first, second, third, fourth)):
        by_group[(group + 4 - d) % 4] = piece[...]


def shifted(value, by):
    return lax.ppermute(value, "mlp", [(i, (i + by) % 4) for i in range(4)])


def exchange(*pieces):
    return [pieces[0]] + [shifted(pieces[d], d) for d in (1, 2, 3)]


RECEIVED = [(144, 768)] * 4


def norm_kernel(group, x, present, validity, gain, shift, first, second, third, fourth, rows, by_group):
    values = []
    for s in range(4):
        rows[...] = jnp.zeros_like(rows)
        normed, _ = standard(widen(rows, x.at[s]))
        rows[...] = (normed * gain[...] + shift[...]) * present[144 * s : 144 * s + 144]
        for i in range(3):
            for m in range(4):
                rows[PAD * i + LON : PAD * i + LON + 1, 192 * m : 192 * m + PAD] = validity[
                    3 * s + i : 3 * s + i + 1, :
                ]
        values.append(rows[...].astype(bf16))
    pack(values, by_group)
    send(group[0], by_group, first, second, third, fourth)


def norm_pack(group, inputs, present, validity, gain, shift):
    return pl.pallas_call(
        norm_kernel,
        in_specs=[SMEM] + [VMEM] * 5,
        out_shape=PIECES,
        scratch_shapes=[pltpu.VMEM((144, 768), f32), GROUPS],
        compiler_params=ROOM,
        cost_estimate=cost(10),
    )(group, inputs, present, validity, gain, shift)


def columns_kernel(group, table, first, second, third, fourth, out, by_group):
    receive(group[0], first, second, third, fourth, by_group)
    out[...] = mm(table[...], by_group[...].reshape(576, 768)).astype(bf16)


def kept_columns_kernel(group, table, first, second, third, fourth, out, kept):
    receive(group[0], first, second, third, fourth, kept)
    out[...] = mm(table[...], kept[...].reshape(576, 768)).astype(bf16)


def to_columns_and_keep(group, table, pieces):
    return pl.pallas_call(
        kept_columns_kernel,
        in_specs=[SMEM] + [VMEM] * 5,
        out_shape=[struct((768, 768), bf16), struct((4, 144, 768), bf16)],
        compiler_params=ROOM,
        cost_estimate=cost(2),
    )(group, table, *pieces)


def validity_kernel(kept, out):
    rows = []
    for s in range(4):
        parts = []
        for m in range(4):
            for i in range(3):
                part = kept[m].astype(f32)[PAD * i + LON : PAD * i + LON + 1, 192 * s : 192 * s + PAD]
                parts.append(part)
        rows.append(jnp.concatenate(parts, axis=1))
    out[...] = jnp.concatenate(rows + [jnp.zeros((4, 576), f32)], axis=0).astype(bf16)


def whole_validity(kept):
    return pl.pallas_call(
        validity_kernel,
        out_shape=struct((8, 576), bf16),
        compiler_params=ROOM,
        cost_estimate=cost(2),
    )(kept)


def to_columns(group, table, pieces):
    return pl.pallas_call(
        columns_kernel,
        in_specs=[SMEM] + [VMEM] * 5,
        out_shape=struct((768, 768), bf16),
        scratch_shapes=[GROUPS],
        cost_estimate=cost(2),
        compiler_params=ROOM,
    )(group, table, *pieces)


def pieces_kernel(group, table, columns, first, second, third, fourth, by_group):
    by_group[...] = mm(table[...], columns[...]).astype(bf16).reshape(4, 144, 768)
    send(group[0], by_group, first, second, third, fourth)


def to_pieces(group, table, columns):
    return pl.pallas_call(
        pieces_kernel,
        in_specs=[SMEM] + [VMEM] * 2,
        out_shape=PIECES,
        scratch_shapes=[GROUPS],
        cost_estimate=cost(2),
        compiler_params=ROOM,
    )(group, table, columns)


def pieces_sums_kernel(
    group, table, columns, kept, validity, gain, shift, first, second, third, fourth, sums, by_group
):
    grad = mm(table[...], columns[...]).astype(bf16)
    by_group[...] = grad.reshape(4, 144, 768)
    send(group[0], by_group, first, second, third, fourth)
    plain = mm(validity[...], grad)
    full = jnp.sum(kept[...].reshape(576, 768).astype(f32) * grad.astype(f32), axis=0, keepdims=True)
    plain = sum(plain[s : s + 1, 192 * s : 192 * s + 192] for s in range(4))
    full = sum(full[:, 192 * s : 192 * s + 192] for s in range(4))
    sums[...] = jnp.zeros_like(sums)
    for k in range(4):

        @pl.when(group[0] == k)
        def _():
            here = slice(192 * k, 192 * k + 192)
            sums[0:1, here] = (full - shift[:, here] * plain) / gain[:, here]
            sums[1:2, here] = plain


def to_pieces_and_sums(group, table, columns, kept, validity, gain, shift):
    outs = pl.pallas_call(
        pieces_sums_kernel,
        in_specs=[SMEM] + [VMEM] * 6,
        out_shape=PIECES + [struct((2, 768), f32)],
        scratch_shapes=[GROUPS],
        compiler_params=ROOM,
        cost_estimate=cost(3),
    )(group, table, columns, kept, validity, gain, shift)
    return outs[:4], outs[4]


def mix_kernel(w_in, w_out, mask, mix_in, mix_out):
    for source, out in ((w_in, mix_in), (w_out, mix_out)):
        parts = []
        for part in range(2):
            row = jnp.concatenate([source[part, 0], source[part, 1]], axis=1)
            row = jnp.concatenate([row, row], axis=1)
            parts.append(jnp.concatenate([row] * 4, axis=0) * mask[...])
        out[:384, :384] = parts[0]
        out[384:, 384:] = parts[0]
        out[:384, 384:] = parts[1]
        out[384:, :384] = -parts[1]


def mixers(w_in, w_out, mask):
    return pl.pallas_call(
        mix_kernel,
        out_shape=[struct((768, 768), bf16)] * 2,
        cost_estimate=cost(1),
        compiler_params=ROOM,
    )(w_in, w_out, mask)


def table_kernel(table, rows, out):
    out[...] = mm(table[...], rows[...]).astype(bf16)


def transform(table, rows):
    return pl.pallas_call(
        table_kernel,
        grid=(3,),
        in_specs=[pl.BlockSpec((384, 1152), lambda t: (t, 0)), whole((1152, 384))],
        out_specs=pl.BlockSpec((384, 384), lambda t: (t, 0)),
        out_shape=struct((1152, 384), bf16),
        compiler_params=ROOM,
    )(table, rows)


def turn(value):
    return jnp.concatenate(
        [
            jnp.concatenate([value[:288, at : at + 384], value[288:, at : at + 384]], axis=1)
            for at in (0, 384)
        ],
        axis=0,
    )


def filter_kernel(
    columns, fwd, inv, mix_in, mix_out, bias_in, bias_out, back, low, first, active, second
):
    grid = turn(mm(fwd[...], columns[...]).astype(bf16))
    low[...] = grid
    value = mm(grid, mix_in[...]) + bias_in[...]
    first[...] = value
    half, _ = gelu_parts(value)
    hot = (value * half).astype(bf16)
    active[...] = hot
    value = mm(hot, mix_out[...]) + bias_out[...]
    second[...] = value
    value = value - SHRINK * value * lax.rsqrt(value * value + SHRINK * SHRINK)
    back[...] = mm(inv[...], turn(value.astype(bf16))).astype(bf16)


def filter_forward(columns, fwd, inv, mix_in, mix_out, bias_in, bias_out):
    return pl.pallas_call(
        filter_kernel,
        out_shape=[
            struct((768, 768), bf16),
            struct((576, 768), bf16),
            struct((576, 768), f32),
            struct((576, 768), bf16),
            struct((576, 768), f32),
        ],
        cost_estimate=cost(150),
        compiler_params=ROOM,
    )(columns, fwd, inv, mix_in, mix_out, bias_in, bias_out)


def filter_back_kernel(
    columns, inv_t, fwd_t, mix_in, mix_out, low, first, active, second, mask, fold, place,
    back, sums, share,
):
    grad = turn(mm(inv_t[...], columns[...]))
    value = second[...]
    root = lax.rsqrt(value * value + SHRINK * SHRINK)
    grad = grad * (1.0 - SHRINK * SHRINK * SHRINK * root * root * root)
    sums[1:2, :] = jnp.sum(grad, axis=0, keepdims=True)
    second_low = grad.astype(bf16)
    value = first[...]
    half, bell = gelu_parts(value)
    grad = outer_cols(second_low, mix_out[...]) * (half + value * bell)
    sums[0:1, :] = jnp.sum(grad, axis=0, keepdims=True)
    first_low = grad.astype(bf16)
    for which, (left, right) in enumerate(((low, first_low), (active, second_low))):
        grad = inner_rows(left[...], right)
        real = grad[:384, :384] + grad[384:, 384:]
        imag = grad[:384, 384:] - grad[384:, :384]
        for part, value in enumerate((real, imag)):
            value = value * mask[...].astype(f32)
            blocks = mm((value[:192] + value[192:]).astype(bf16), fold[...]).astype(bf16)
            for piece in range(3):
                at = which * 384 + part * 192 + piece * 64
                group, row = at // 128, at % 128
                share[row : row + 64, group * 128 : group * 128 + 128] = blocks[
                    piece * 64 : piece * 64 + 64
                ]
    grad = turn(outer_cols(first_low, mix_in[...]).astype(bf16))
    back[...] = (mm(fwd_t[...], grad) + mm(place[...], share[...])).astype(bf16)


def filter_backward(*operands):
    return pl.pallas_call(
        filter_back_kernel,
        out_shape=[struct((768, 768), bf16), struct((2, 768), f32)],
        scratch_shapes=[pltpu.VMEM((128, 768), bf16)],
        cost_estimate=cost(57),
        compiler_params=ROOM,
    )(*operands)


def prepare_kernel(x, present, cotangent, gain, shift, w_out, base, grad_low, back, sums, rows):
    @pl.when(pl.program_id(0) == 0)
    def _():
        rows[...] = jnp.zeros_like(rows)
        bias_sum = jnp.zeros((1, 768), f32)
        for s in range(4):
            here = slice(144 * s, 144 * s + 144)
            there = present[here]
            value = widen(rows, x.at[s])
            normed, _ = standard(value)
            base[here] = value + (normed * gain[...] + shift[...]) * there
            value = widen(rows, cotangent.at[s]) * there
            bias_sum += jnp.sum(value, axis=0, keepdims=True)
            grad_low[here] = value.astype(bf16)
        sums[...] = bias_sum

    back[0] = outer_cols(grad_low[...], w_out[...].reshape(768, 768))


def prepare(x, present, cotangent, gain, shift, weights):
    return pl.pallas_call(
        prepare_kernel,
        grid=(4,),
        in_specs=[
            whole((4, 3, LON, 768)),
            whole((576, 1)),
            whole((4, 3, LON, 768)),
            whole((1, 768)),
            whole((1, 768)),
            pl.BlockSpec((16, 1, PAD, 768), lambda g: (1, g, 0, 0)),
        ],
        out_specs=[
            whole((576, 768)),
            whole((576, 768)),
            pl.BlockSpec((1, 576, 768), lambda g: (g, 0, 0)),
            whole((1, 768)),
        ],
        out_shape=[
            struct((576, 768), f32),
            struct((576, 768), bf16),
            struct((4, 576, 768), f32),
            struct((1, 768), f32),
        ],
        scratch_shapes=[pltpu.VMEM((144, 768), f32)],
        compiler_params=ROOM,
        cost_estimate=cost(6),
    )(x, present, cotangent, gain, shift, weights)


def chain_kernel(
    at, base, in1, in2, in3, in4, cotangent, gain, shift, w_in, back, units,
    stream, mixed, hidden, grad_pre, grad_stream, out1, out2, out3, out4, sums, unit_sums,
    rows, normed, scale, total, by_group,
):
    step = pl.program_id(0)

    @pl.when(step == 0)
    def _():
        rows[...] = jnp.zeros_like(rows)
        total[...] = jnp.zeros_like(total)
        receive(at[0], in1, in2, in3, in4, by_group)
        for s in range(4):
            here = slice(144 * s, 144 * s + 144)
            value = base[here] + unpack(by_group, s)
            stream[here] = value
            value, spread_of = standard(value.astype(bf16).astype(f32))
            normed[here] = value
            scale[here] = spread_of
            mixed[here] = (value * gain[...] + shift[...]).astype(bf16)

    into = w_in[...].reshape(768, 768)
    value = mm(mixed[...], into) + units[0]
    half, bell = gelu_parts(value)
    hidden[0] = (value * half).astype(bf16)
    grad = back[0] * (half + value * bell)
    unit_sums[0] = jnp.sum(grad, axis=0, keepdims=True)
    grad = grad.astype(bf16)
    grad_pre[0] = grad
    total[...] += outer_cols(grad, into).astype(bf16).astype(f32)

    @pl.when(step == 3)
    def _():
        lows = []
        norm_sum = jnp.zeros((1, 768), f32)
        plain_sum = jnp.zeros((1, 768), f32)
        for s in range(4):
            here = slice(144 * s, 144 * s + 144)
            grad = total[here]
            value = normed[here]
            norm_sum += jnp.sum(grad * value, axis=0, keepdims=True)
            plain_sum += jnp.sum(grad, axis=0, keepdims=True)
            grad = grad * gain[...]
            grad = grad - jnp.mean(grad, axis=-1, keepdims=True) - value * jnp.mean(
                grad * value, axis=-1, keepdims=True
            )
            grad = widen(rows, cotangent.at[s]) + scale[here] * grad
            grad_stream[here] = grad
            lows.append(grad.astype(bf16))
        sums[0:1, :] = norm_sum
        sums[1:2, :] = plain_sum
        pack(lows, by_group)
        send(at[0], by_group, out1, out2, out3, out4)


def chain(group, base, pieces, cotangent, gain, shift, weights, back, units):
    by_step = pl.BlockSpec((1, 576, 768), lambda g: (g, 0, 0))
    outs = pl.pallas_call(
        chain_kernel,
        grid=(4,),
        in_specs=[
            SMEM,
            whole((576, 768)),
            *[whole(shape) for shape in RECEIVED],
            whole((4, 3, LON, 768)),
            whole((1, 768)),
            whole((1, 768)),
            pl.BlockSpec((16, 1, PAD, 768), lambda g: (0, g, 0, 0)),
            by_step,
            pl.BlockSpec((1, 1, 768), lambda g: (g, 0, 0)),
        ],
        out_specs=[
            *[whole((576, 768))] * 2,
            by_step,
            by_step,
            whole((576, 768)),
            *[whole(piece.shape) for piece in PIECES],
            whole((2, 768)),
            pl.BlockSpec((1, 1, 768), lambda g: (g, 0, 0)),
        ],
        out_shape=[
            struct((576, 768), f32),
            struct((576, 768), bf16),
            struct((4, 576, 768), bf16),
            struct((4, 576, 768), bf16),
            struct((576, 768), f32),
            *PIECES,
            struct((2, 768), f32),
            struct((4, 1, 768), f32),
        ],
        scratch_shapes=[
            pltpu.VMEM((144, 768), f32),
            pltpu.VMEM((576, 768), f32),
            pltpu.VMEM((576, 1), f32),
            pltpu.VMEM((576, 768), f32),
            GROUPS,
        ],
        compiler_params=ROOM,
        cost_estimate=cost(14),
    )(group, base, *pieces, cotangent, gain, shift, weights, back, units)
    return outs[:5], outs[5:9], outs[9], outs[10]


def share_kernel(core, mixed, grad_pre, hidden, grad_low, *rest):
    own = len(rest) == 2
    out = rest[-1]

    def store(value):
        value = value.reshape(16, 1, PAD, 768)
        if own:
            value = value + rest[0][...].astype(f32)
        out[...] = value.astype(bf16)

    @pl.when(core[0] == (0 if own else 1))
    def _():
        store(inner_rows(mixed[...], grad_pre[0]))

    @pl.when(core[0] == (1 if own else 0))
    def _():
        store(inner_rows(hidden[0], grad_low[...]))


def weight_share(core, mixed, grad_pre, hidden, grad_low, *given):
    by_step = pl.BlockSpec((1, 576, 768), lambda g: (g, 0, 0))
    pieces = pl.BlockSpec((16, 1, PAD, 768), lambda g: (0, g, 0, 0))
    return pl.pallas_call(
        share_kernel,
        grid=(4,),
        in_specs=[SMEM, whole((576, 768)), by_step, by_step, whole((576, 768))] + [pieces] * len(given),
        out_specs=pieces,
        out_shape=struct((16, 4, PAD, 768), bf16),
        compiler_params=ROOM,
        cost_estimate=cost(7),
    )(core, mixed, grad_pre, hidden, grad_low, *given)


def output_kernel(hidden, w_out, stream, present, bias, x, grad_stream, out, sums, total, rows):
    step = pl.program_id(0)
    part = mm(hidden[0], w_out[...].reshape(768, 768)).astype(bf16).astype(f32)

    @pl.when(step == 0)
    def _():
        total[...] = part

    @pl.when(step > 0)
    def _():
        total[...] += part

    @pl.when(step == 3)
    def _():
        rows[...] = jnp.zeros_like(rows)
        norm_sum = jnp.zeros((1, 768), f32)
        plain_sum = jnp.zeros((1, 768), f32)
        for s in range(4):
            here = slice(144 * s, 144 * s + 144)
            value = stream[here] + present[here] * (total[here] + bias[...])
            for i in range(3):
                out[s, i] = value[PAD * i : PAD * i + LON].astype(bf16)
            normed, _ = standard(widen(rows, x.at[s]))
            grad = grad_stream[here] * present[here]
            norm_sum += jnp.sum(grad * normed, axis=0, keepdims=True)
            plain_sum += jnp.sum(grad, axis=0, keepdims=True)
        sums[0:1, :] = norm_sum
        sums[1:2, :] = plain_sum


def layer_output(hidden, weights, stream, present, bias, x, grad_stream):
    return pl.pallas_call(
        output_kernel,
        grid=(4,),
        in_specs=[
            pl.BlockSpec((1, 576, 768), lambda g: (g, 0, 0)),
            pl.BlockSpec((16, 1, PAD, 768), lambda g: (1, g, 0, 0)),
            whole((576, 768)),
            whole((576, 1)),
            whole((1, 768)),
            whole((4, 3, LON, 768)),
            whole((576, 768)),
        ],
        out_specs=[whole((4, 3, LON, 768)), whole((2, 768))],
        out_shape=[struct((4, 3, LON, 768), bf16), struct((2, 768), f32)],
        scratch_shapes=[pltpu.VMEM((576, 768), f32), pltpu.VMEM((144, 768), f32)],
        compiler_params=ROOM,
        cost_estimate=cost(10),
    )(hidden, weights, stream, present, bias, x, grad_stream)


def final_kernel(group, x, present, grad_stream, gain, first, second, third, fourth, out, rows, by_group):
    rows[...] = jnp.zeros_like(rows)
    receive(group[0], first, second, third, fourth, by_group)
    for s in range(4):
        here = slice(144 * s, 144 * s + 144)
        normed, scale = standard(widen(rows, x.at[s]))
        stream = grad_stream[here]
        grad = (unpack(by_group, s) + stream) * present[here] * gain[...]
        grad = grad - jnp.mean(grad, axis=-1, keepdims=True) - normed * jnp.mean(
            grad * normed, axis=-1, keepdims=True
        )
        grad = stream + scale * grad
        for i in range(3):
            out[s, i] = grad[PAD * i : PAD * i + LON]


def input_grads(group, x, present, grad_stream, gain, pieces):
    return pl.pallas_call(
        final_kernel,
        in_specs=[SMEM] + [VMEM] * 8,
        out_shape=struct((4, 3, LON, 768), f32),
        scratch_shapes=[pltpu.VMEM((144, 768), f32), GROUPS],
        compiler_params=ROOM,
        cost_estimate=cost(20),
    )(group, x, present, grad_stream, gain, *pieces)


def share_sum_kernel(own, first, second, third, out):
    rows = [piece[...].astype(f32) for piece in (own, first, second, third)]
    out[...] = (rows[0] + rows[1] + rows[2] + rows[3]).astype(bf16)


def small_sum_kernel(own, first, second, third, out):
    rows = [piece[...].astype(f32) for piece in (own, first, second, third)]
    value = jnp.concatenate(
        [(rows[0] + rows[1] + rows[2] + rows[3])[:6]]
        + [row[6:7] for row in rows]
        + [row[7:11] for row in rows]
        + [jnp.zeros((6, 768), f32)],
        axis=0,
    )
    out[...] = value.astype(bf16)


def over_groups(kernel, count, rows):
    return pl.pallas_call(
        kernel,
        out_shape=struct((count, 768), bf16),
        compiler_params=ROOM,
        cost_estimate=cost(1),
    )(rows[0], *(shifted(rows[d], 4 - d) for d in (1, 2, 3)))


def copies_kernel(one, other, out):
    value = (one[...].astype(f32) + other[...].astype(f32)).astype(bf16)
    for q in range(16):
        out[q] = value


def over_snapshots(rows):
    return pl.pallas_call(
        copies_kernel,
        out_shape=struct((16,) + rows.shape, bf16),
        compiler_params=ROOM,
        cost_estimate=cost(1),
    )(rows, lax.ppermute(rows, "dp", [(0, 1), (1, 0)]))


def finish_kernel(at, own, other, own_small, other_small, w_in, w_out, f_in, f_out, small, biases, joined):
    core, group = at[0], at[1]
    own_rest = own_small[...].astype(f32)
    other_rest = other_small[...].astype(f32)

    for k, (zero, one) in enumerate(((own_rest, other_rest), (other_rest, own_rest))):

        @pl.when(core == k)
        def _():
            (w_in, w_out)[k][...] = own[...].reshape(768, 768).astype(f32)
            (w_in, w_out)[1 - k][...] = other[...].reshape(768, 768).astype(f32)
            for d in range(4):
                joined[d, :, :4] = zero[:, 10 + 4 * d : 14 + 4 * d]
                joined[d, :, 4:] = one[:, 10 + 4 * d : 14 + 4 * d]

    sums = jnp.sum(own_rest + other_rest, axis=0)
    for d in range(4):
        m = (group + d) % 4
        rows = joined[d].reshape(128, 768)
        biases[pl.ds(m, 1), :] = sums[6 + d : 7 + d]
        for which, out in enumerate((f_in, f_out)):
            for part in range(2):
                for b in range(2):
                    pieces = []
                    for piece in range(3):
                        row = which * 384 + part * 192 + b * 96 + piece * 32
                        u, row = row // 128, row % 128
                        pieces.append(rows[row : row + 32, 128 * u : 128 * u + 128])
                    out[part, 2 * m + b] = jnp.concatenate(pieces, axis=0)[:, :96]
    small[...] = sums[:8]


def finish(at, *rows):
    return pl.pallas_call(
        finish_kernel,
        in_specs=[SMEM] + [VMEM] * 4,
        out_shape=[
            struct((768, 768), f32),
            struct((768, 768), f32),
            struct((2, 8, 96, 96), f32),
            struct((2, 8, 96, 96), f32),
            struct((8, 768), f32),
            struct((4, 768), f32),
        ],
        scratch_shapes=[pltpu.VMEM((4, 16, 8, 768), f32)],
        compiler_params=ROOM,
        cost_estimate=cost(5),
    )(at, *rows)


def swap(value, axes):
    return lax.all_to_all(value, axes, 0, 0, tiled=True)


def across(columns):
    return swap(columns.reshape(32, 24, 768), WIDE).reshape(768, 768)


def after(value, *others):
    return lax.optimization_barrier((value,) + others)[0]


def shards(
    inputs,
    validity,
    gain_first,
    shift_first,
    spectral_in,
    spectral_in_bias,
    spectral_out,
    spectral_out_bias,
    gain_second,
    shift_second,
    weight_in,
    bias_in,
    weight_out,
    bias_out,
    cotangent,
):
    core = lax.axis_index("core")
    group = lax.axis_index("mlp")
    table = {name: jnp.asarray(value) for name, value in tables().items()}
    mask, fold = (jnp.asarray(value) for value in block_fold())
    gain_first, shift_first, gain_second, shift_second, bias_out = (
        value.reshape(1, 768)
        for value in (gain_first, shift_first, gain_second, shift_second, bias_out)
    )

    present = jnp.pad(validity.astype(f32), ((0, 0), (0, 0), (0, PAD - LON))).reshape(576, 1)
    here = group.astype(jnp.int32).reshape(1)
    lanes = jnp.pad(validity.astype(f32).reshape(12, LON), ((0, 0), (0, PAD - LON)))
    tokens = exchange(*norm_pack(here, inputs, present, lanes, gain_first, shift_first))

    wide = lax.axis_index(WIDE)
    high = lax.reduce_precision(bias_in, 8, 7)
    middle = lax.reduce_precision(bias_in - high, 8, 7)
    bias_rows = jnp.stack([high, middle, bias_in - high - middle]).astype(bf16)
    both = jnp.concatenate([weight_in, weight_out], axis=0)
    piece = jnp.concatenate(
        [
            lax.dynamic_slice_in_dim(both, wide * PAD, PAD, 0),
            bias_rows,
            jnp.zeros((13, 768), bf16),
        ]
    )
    pieces = jnp.stack([piece] + [shifted(piece, d) for d in (1, 2, 3)])
    weights = lax.all_gather(pieces[:, :PAD], WIDE)
    units = pieces[:, PAD : PAD + 3].astype(f32)
    units = (units[:, 0] + units[:, 1] + units[:, 2]).reshape(4, 1, 768)

    mix_in, mix_out = mixers(spectral_in, spectral_out, mask)
    mix_in_bias, mix_out_bias = (
        jnp.tile(value.reshape(2, 1, 192), (1, 2, 1)).reshape(1, 768)
        for value in (spectral_in_bias, spectral_out_bias)
    )

    columns, kept = to_columns_and_keep(here, table["lon_fwd"], tokens)
    columns = across(columns)
    row_validity = whole_validity(kept)
    back, low, first, active, second = filter_forward(
        columns, table["grid_fwd"], table["grid_inv"], mix_in, mix_out, mix_in_bias, mix_out_bias
    )
    filtered = exchange(*to_pieces(here, table["lon_inv"], across(back)))
    base, grad_low, grad_hidden, bias_sum = prepare(
        inputs, present, cotangent, gain_first, shift_first, weights
    )
    (stream, mixed, hidden, grad_pre, grad_stream), sent, sums, unit_sums = chain(
        here, base, filtered, cotangent, gain_second, shift_second, weights, grad_hidden, units
    )
    operands = (core.astype(jnp.int32).reshape(1), mixed, grad_pre, hidden, grad_low)
    share = weight_share(*operands)
    share = weight_share(*operands, lax.ppermute(share, "core", [(0, 1), (1, 0)]))
    output, first_sums = layer_output(
        hidden, weights, after(stream, share), present, bias_out, inputs, grad_stream
    )
    share = lax.psum_scatter(share.reshape(3072, 768), XY, scatter_dimension=0, tiled=True)

    columns = after(across(to_columns(here, table["lon_inv_t"], exchange(*sent))), output)
    back, filter_sums = filter_backward(
        columns,
        table["grid_inv_t"],
        table["grid_fwd_t"],
        mix_in,
        mix_out,
        low,
        first,
        active,
        second,
        mask,
        fold,
        table["place"],
    )
    back = across(back)
    filter_share = jnp.sum(back.reshape(32, 24, 768)[:, 18:22].astype(f32), axis=0).astype(bf16)
    sent, piece_sums = to_pieces_and_sums(
        here, table["lon_fwd_t"], back, kept, row_validity, gain_first, shift_first
    )
    grad_inputs = input_grads(here, inputs, present, grad_stream, gain_first, exchange(*sent))

    filter_sums = jnp.sum(filter_sums.reshape(2, 2, 2, 192), axis=2).reshape(1, 768)
    rest = jnp.concatenate([first_sums + piece_sums, sums, bias_sum, filter_sums]).astype(bf16)
    rest = jnp.concatenate([rest, filter_share, jnp.zeros((5, 768), bf16)])
    unit_sums = unit_sums.reshape(4, 1, 768).astype(bf16)
    rest = [jnp.concatenate([unit_sums[d], rest]) for d in range(4)]
    rest = swap(over_snapshots(over_groups(small_sum_kernel, 32, rest)), XY)
    share = share.reshape(4, PAD, 768)
    share = over_groups(share_sum_kernel, PAD, [share[d] for d in range(4)])
    share = swap(over_snapshots(share), XY)
    pair = [(0, 1), (1, 0)]
    grad_w_in, grad_w_out, grad_f_in, grad_f_out, small, biases = finish(
        jnp.stack([core, group]).astype(jnp.int32),
        share,
        lax.ppermute(share, "core", pair),
        rest,
        lax.ppermute(rest, "core", pair),
    )
    biases = biases.reshape(4, 2, 2, 2, 96).transpose(1, 2, 0, 3, 4).reshape(2, 2, 8, 96)
    mine = lax.dynamic_slice_in_dim(small[1:6], group * 192, 192, 1)
    return (
        output,
        grad_inputs,
        mine[0],
        mine[1],
        grad_f_in,
        biases[0],
        grad_f_out,
        biases[1],
        mine[2],
        mine[3],
        grad_w_in,
        small[0],
        grad_w_out,
        mine[4],
    )


def solution(mesh):
    fine = Mesh(mesh.devices.reshape(2, 4, 4, 2, 4), EVERY)
    tokens = P("dp", ("x", "y", "core"), "mlp")
    placed = (
        tokens,
        tokens,
        P(),
        P(),
        P(None, "mlp"),
        P(None, "mlp"),
        P(None, "mlp"),
        P(None, "mlp"),
        P(),
        P(),
        P(None, "mlp"),
        P("mlp"),
        P("mlp", None),
        P(),
        tokens,
    )
    return jax.shard_map(
        shards,
        mesh=fine,
        in_specs=placed,
        out_specs=(
            tokens,
            tokens,
            P("mlp"),
            P("mlp"),
            P(),
            P(),
            P(),
            P(),
            P("mlp"),
            P("mlp"),
            P(None, "mlp"),
            P("mlp"),
            P("mlp", None),
            P("mlp"),
        ),
        check_vma=False,
    )
```

```python
import math

import jax
import jax.numpy as jnp
import numpy as np
from jax import lax
from jax.experimental import pallas as pl
from jax.experimental.pallas import tpu as pltpu
from jax.sharding import Mesh
from jax.sharding import PartitionSpec as P

H = 96
KWP = 96
W = 180
LON = 45
PAD = 48
EPSILON = 1e-05
SHRINK = 0.01
ROOT_HALF = math.sqrt(0.5)
ROOT_TWO_PI = math.sqrt(2.0 * math.pi)

XY = ("x", "y")
WIDE = ("x", "y", "core")
EVERY = ("dp", "x", "y", "core", "mlp")
bf16 = jnp.bfloat16
f32 = jnp.float32
ROOM = pltpu.CompilerParams(vmem_limit_bytes=50 * 1024 * 1024)


def tables():
    w = np.arange(W)
    k = np.arange(KWP)
    phase = 2.0 * np.pi * ((w[:, None] * k[None, :]) % W) / W
    live = np.where(k < W // 2 + 1, 1.0 / math.sqrt(W), 0.0)
    weight = np.where((k == 0) | (2 * k == W), 1.0, 2.0) * live
    fwd = np.stack([np.cos(phase) * live, -np.sin(phase) * live], axis=2)
    inv = np.stack([np.cos(phase) * weight, -np.sin(phase) * weight], axis=2)
    pad = ((0, 0), (0, PAD - LON), (0, 0), (0, 0))
    fwd = np.pad(fwd.reshape(4, LON, KWP, 2), pad).reshape(4, PAD, 32, 3, 2)
    inv = np.pad(inv.reshape(4, LON, KWP, 2), pad).reshape(4, PAD, 32, 3, 2)
    eye = np.eye(3)

    def columns(table):
        table = table.reshape(32, 18, -1)
        return np.pad(table, ((0, 0), (0, 6), (0, 0))).reshape(768, -1)

    lon_fwd = columns(np.einsum("mwvkp,ia->vakpmiw", fwd, eye))
    lon_inv = columns(np.einsum("mwvkp,ia->vakpmiw", inv, eye))
    h = np.arange(H)
    angle = 2.0 * np.pi * ((h[:, None] * h[None, :]) % H) / H
    cos = np.cos(angle) / math.sqrt(H)
    sin = np.sin(angle) / math.sqrt(H)
    lat_fwd = np.stack([np.stack([cos, sin]), np.stack([-sin, cos])])
    lat_inv = np.stack([np.stack([cos, -sin]), np.stack([sin, cos])])
    grid_fwd = columns(np.einsum("pqjva,kl->valqpkj", lat_fwd.reshape(2, 2, H, 32, 3), eye))
    grid_inv = columns(np.einsum("pqvaj,kl->valpqkj", lat_inv.reshape(2, 2, 32, 3, H), eye))

    def low(table):
        return np.ascontiguousarray(table).astype(np.float32).astype(bf16)

    return {
        "lon_fwd": low(lon_fwd),
        "lon_inv": low(lon_inv.T),
        "lon_fwd_t": low(lon_fwd.T),
        "lon_inv_t": low(lon_inv),
        "grid_fwd": low(grid_fwd.T),
        "grid_inv": low(grid_inv),
        "grid_fwd_t": low(grid_fwd),
        "grid_inv_t": low(grid_inv.T),
        "place": low(np.pad(np.eye(128).reshape(32, 4, 128), ((0, 0), (18, 2), (0, 0))).reshape(768, 128)),
    }


def block_fold():
    at = np.arange(384) // 96
    mask = (at[:, None] == at[None, :]).astype(np.float32)
    fold = np.tile(np.eye(96, 128), (4, 1)).astype(np.float32)
    return mask.astype(bf16), fold.astype(bf16)


def mm(left, right):
    return jnp.dot(left, right, preferred_element_type=f32)


def inner_rows(left, right):
    return lax.dot_general(left, right, (((0,), (0,)), ((), ())), preferred_element_type=f32)


def outer_cols(left, right):
    return lax.dot_general(left, right, (((1,), (1,)), ((), ())), preferred_element_type=f32)


def gelu_parts(value):
    half = 0.5 * (1.0 + lax.erf(value * ROOT_HALF))
    return half, jnp.exp(-0.5 * value * value) * (1.0 / ROOT_TWO_PI)


def standard(value):
    centred = value - jnp.mean(value, axis=-1, keepdims=True)
    scale = lax.rsqrt(jnp.mean(centred * centred, axis=-1, keepdims=True) + EPSILON)
    return centred * scale, scale


def widen(rows, source):
    for i in range(3):
        rows[PAD * i : PAD * i + LON, :] = source[i].astype(f32)
    return rows[...]


def cost(us):
    return pl.CostEstimate(flops=us * 1100000000, bytes_accessed=us * 1000000, transcendentals=0)


def group_weight(own, others):
    return jnp.where(pl.program_id(0) == 0, own[...], others[...].reshape(768, 768))


def others_weight(which):
    return pl.BlockSpec((16, 1, PAD, 768), lambda g: (which, jnp.maximum(g - 1, 0), 0, 0))


def whole(shape):
    return pl.BlockSpec(shape, lambda *_: (0,) * len(shape))


def struct(shape, dtype):
    return jax.ShapeDtypeStruct(shape, dtype)


PIECES = [struct((144, 768), bf16)] * 4
GROUPS = pltpu.VMEM((4, 144, 768), bf16)
SMEM = pl.BlockSpec(memory_space=pltpu.SMEM)
VMEM = pl.BlockSpec(memory_space=pltpu.VMEM)


def pack(values, by_group):
    for m in range(4):
        here = slice(192 * m, 192 * m + 192)
        by_group[m] = jnp.concatenate([value[:, here] for value in values], axis=1)


def unpack(by_group, s):
    here = slice(192 * s, 192 * s + 192)
    return jnp.concatenate([by_group[m][:, here] for m in range(4)], axis=1).astype(f32)


def send(group, by_group, *outs):
    for d in range(4):
        outs[d][...] = by_group[(group + d) % 4]


def receive(group, first, second, third, fourth, by_group):
    for d, piece in enumerate((first, second, third, fourth)):
        by_group[(group + 4 - d) % 4] = piece[...]


def shifted(value, by):
    return lax.ppermute(value, "mlp", [(i, (i + by) % 4) for i in range(4)])


def exchange(*pieces):
    return [pieces[0]] + [shifted(pieces[d], d) for d in (1, 2, 3)]


RECEIVED = [(144, 768)] * 4


def norm_kernel(group, x, present, validity, gain, shift, first, second, third, fourth, rows, by_group):
    values = []
    for s in range(4):
        rows[...] = jnp.zeros_like(rows)
        normed, _ = standard(widen(rows, x.at[s]))
        rows[...] = (normed * gain[...] + shift[...]) * present[144 * s : 144 * s + 144]
        for i in range(3):
            for m in range(4):
                rows[PAD * i + LON : PAD * i + LON + 1, 192 * m : 192 * m + PAD] = validity[
                    3 * s + i : 3 * s + i + 1, :
                ]
        values.append(rows[...].astype(bf16))
    pack(values, by_group)
    send(group[0], by_group, first, second, third, fourth)


def norm_pack(group, inputs, present, validity, gain, shift):
    return pl.pallas_call(
        norm_kernel,
        in_specs=[SMEM] + [VMEM] * 5,
        out_shape=PIECES,
        scratch_shapes=[pltpu.VMEM((144, 768), f32), GROUPS],
        compiler_params=ROOM,
        cost_estimate=cost(10),
    )(group, inputs, present, validity, gain, shift)


def columns_kernel(group, table, first, second, third, fourth, out, by_group):
    receive(group[0], first, second, third, fourth, by_group)
    out[...] = mm(table[...], by_group[...].reshape(576, 768)).astype(bf16)


def kept_columns_kernel(group, table, first, second, third, fourth, out, kept):
    receive(group[0], first, second, third, fourth, kept)
    out[...] = mm(table[...], kept[...].reshape(576, 768)).astype(bf16)


def to_columns_and_keep(group, table, pieces):
    return pl.pallas_call(
        kept_columns_kernel,
        in_specs=[SMEM] + [VMEM] * 5,
        out_shape=[struct((768, 768), bf16), struct((4, 144, 768), bf16)],
        compiler_params=ROOM,
        cost_estimate=cost(2),
    )(group, table, *pieces)


def validity_kernel(kept, out):
    rows = []
    for s in range(4):
        parts = []
        for m in range(4):
            for i in range(3):
                part = kept[m].astype(f32)[PAD * i + LON : PAD * i + LON + 1, 192 * s : 192 * s + PAD]
                parts.append(part)
        rows.append(jnp.concatenate(parts, axis=1))
    out[...] = jnp.concatenate(rows + [jnp.zeros((4, 576), f32)], axis=0).astype(bf16)


def whole_validity(kept):
    return pl.pallas_call(
        validity_kernel,
        out_shape=struct((8, 576), bf16),
        compiler_params=ROOM,
        cost_estimate=cost(2),
    )(kept)


def to_columns(group, table, pieces):
    return pl.pallas_call(
        columns_kernel,
        in_specs=[SMEM] + [VMEM] * 5,
        out_shape=struct((768, 768), bf16),
        scratch_shapes=[GROUPS],
        cost_estimate=cost(2),
        compiler_params=ROOM,
    )(group, table, *pieces)


def pieces_kernel(group, table, columns, first, second, third, fourth, by_group):
    by_group[...] = mm(table[...], columns[...]).astype(bf16).reshape(4, 144, 768)
    send(group[0], by_group, first, second, third, fourth)


def to_pieces(group, table, columns):
    return pl.pallas_call(
        pieces_kernel,
        in_specs=[SMEM] + [VMEM] * 2,
        out_shape=PIECES,
        scratch_shapes=[GROUPS],
        cost_estimate=cost(2),
        compiler_params=ROOM,
    )(group, table, columns)


def pieces_sums_kernel(
    group, table, columns, kept, validity, gain, shift, first, second, third, fourth, sums, by_group
):
    grad = mm(table[...], columns[...]).astype(bf16)
    by_group[...] = grad.reshape(4, 144, 768)
    send(group[0], by_group, first, second, third, fourth)
    plain = mm(validity[...], grad)
    full = jnp.sum(kept[...].reshape(576, 768).astype(f32) * grad.astype(f32), axis=0, keepdims=True)
    plain = sum(plain[s : s + 1, 192 * s : 192 * s + 192] for s in range(4))
    full = sum(full[:, 192 * s : 192 * s + 192] for s in range(4))
    sums[...] = jnp.zeros_like(sums)
    for k in range(4):

        @pl.when(group[0] == k)
        def _():
            here = slice(192 * k, 192 * k + 192)
            sums[0:1, here] = (full - shift[:, here] * plain) / gain[:, here]
            sums[1:2, here] = plain


def to_pieces_and_sums(group, table, columns, kept, validity, gain, shift):
    outs = pl.pallas_call(
        pieces_sums_kernel,
        in_specs=[SMEM] + [VMEM] * 6,
        out_shape=PIECES + [struct((2, 768), f32)],
        scratch_shapes=[GROUPS],
        compiler_params=ROOM,
        cost_estimate=cost(3),
    )(group, table, columns, kept, validity, gain, shift)
    return outs[:4], outs[4]


def mix_kernel(w_in, w_out, mask, mix_in, mix_out):
    for source, out in ((w_in, mix_in), (w_out, mix_out)):
        parts = []
        for part in range(2):
            row = jnp.concatenate([source[part, 0], source[part, 1]], axis=1)
            row = jnp.concatenate([row, row], axis=1)
            parts.append(jnp.concatenate([row] * 4, axis=0) * mask[...])
        out[:384, :384] = parts[0]
        out[384:, 384:] = parts[0]
        out[:384, 384:] = parts[1]
        out[384:, :384] = -parts[1]


def mixers(w_in, w_out, mask):
    return pl.pallas_call(
        mix_kernel,
        out_shape=[struct((768, 768), bf16)] * 2,
        cost_estimate=cost(1),
        compiler_params=ROOM,
    )(w_in, w_out, mask)


def table_kernel(table, rows, out):
    out[...] = mm(table[...], rows[...]).astype(bf16)


def transform(table, rows):
    return pl.pallas_call(
        table_kernel,
        grid=(3,),
        in_specs=[pl.BlockSpec((384, 1152), lambda t: (t, 0)), whole((1152, 384))],
        out_specs=pl.BlockSpec((384, 384), lambda t: (t, 0)),
        out_shape=struct((1152, 384), bf16),
        compiler_params=ROOM,
    )(table, rows)


def turn(value):
    return jnp.concatenate(
        [
            jnp.concatenate([value[:288, at : at + 384], value[288:, at : at + 384]], axis=1)
            for at in (0, 384)
        ],
        axis=0,
    )


def filter_kernel(
    columns, fwd, inv, mix_in, mix_out, bias_in, bias_out, back, low, first, active, second
):
    grid = turn(mm(fwd[...], columns[...]).astype(bf16))
    low[...] = grid
    value = mm(grid, mix_in[...]) + bias_in[...]
    first[...] = value
    half, _ = gelu_parts(value)
    hot = (value * half).astype(bf16)
    active[...] = hot
    value = mm(hot, mix_out[...]) + bias_out[...]
    second[...] = value
    value = value - SHRINK * value * lax.rsqrt(value * value + SHRINK * SHRINK)
    back[...] = mm(inv[...], turn(value.astype(bf16))).astype(bf16)


def filter_forward(columns, fwd, inv, mix_in, mix_out, bias_in, bias_out):
    return pl.pallas_call(
        filter_kernel,
        out_shape=[
            struct((768, 768), bf16),
            struct((576, 768), bf16),
            struct((576, 768), f32),
            struct((576, 768), bf16),
            struct((576, 768), f32),
        ],
        cost_estimate=cost(150),
        compiler_params=ROOM,
    )(columns, fwd, inv, mix_in, mix_out, bias_in, bias_out)


def filter_back_kernel(
    columns, inv_t, fwd_t, mix_in, mix_out, low, first, active, second, mask, fold, place,
    back, sums, share,
):
    grad = turn(mm(inv_t[...], columns[...]))
    value = second[...]
    root = lax.rsqrt(value * value + SHRINK * SHRINK)
    grad = grad * (1.0 - SHRINK * SHRINK * SHRINK * root * root * root)
    sums[1:2, :] = jnp.sum(grad, axis=0, keepdims=True)
    second_low = grad.astype(bf16)
    value = first[...]
    half, bell = gelu_parts(value)
    grad = outer_cols(second_low, mix_out[...]) * (half + value * bell)
    sums[0:1, :] = jnp.sum(grad, axis=0, keepdims=True)
    first_low = grad.astype(bf16)
    for which, (left, right) in enumerate(((low, first_low), (active, second_low))):
        grad = inner_rows(left[...], right)
        real = grad[:384, :384] + grad[384:, 384:]
        imag = grad[:384, 384:] - grad[384:, :384]
        for part, value in enumerate((real, imag)):
            value = value * mask[...].astype(f32)
            blocks = mm((value[:192] + value[192:]).astype(bf16), fold[...]).astype(bf16)
            for piece in range(3):
                at = which * 384 + part * 192 + piece * 64
                group, row = at // 128, at % 128
                share[row : row + 64, group * 128 : group * 128 + 128] = blocks[
                    piece * 64 : piece * 64 + 64
                ]
    grad = turn(outer_cols(first_low, mix_in[...]).astype(bf16))
    back[...] = (mm(fwd_t[...], grad) + mm(place[...], share[...])).astype(bf16)


def filter_backward(*operands):
    return pl.pallas_call(
        filter_back_kernel,
        out_shape=[struct((768, 768), bf16), struct((2, 768), f32)],
        scratch_shapes=[pltpu.VMEM((128, 768), bf16)],
        cost_estimate=cost(61),
        compiler_params=ROOM,
    )(*operands)


def prepare_kernel(x, present, cotangent, gain, shift, base, grad_low, sums, rows):
    rows[...] = jnp.zeros_like(rows)
    bias_sum = jnp.zeros((1, 768), f32)
    for s in range(4):
        here = slice(144 * s, 144 * s + 144)
        there = present[here]
        value = widen(rows, x.at[s])
        normed, _ = standard(value)
        base[here] = value + (normed * gain[...] + shift[...]) * there
        value = widen(rows, cotangent.at[s]) * there
        bias_sum += jnp.sum(value, axis=0, keepdims=True)
        grad_low[here] = value.astype(bf16)
    sums[...] = bias_sum


def prepare(x, present, cotangent, gain, shift):
    return pl.pallas_call(
        prepare_kernel,
        out_shape=[struct((576, 768), f32), struct((576, 768), bf16), struct((1, 768), f32)],
        scratch_shapes=[pltpu.VMEM((144, 768), f32)],
        compiler_params=ROOM,
        cost_estimate=cost(3),
    )(x, present, cotangent, gain, shift)


def chain_kernel(
    at, base, in1, in2, in3, in4, cotangent, grad_low, gain, shift, own, w_in, own_out, w_out, units,
    stream, mixed, hidden, grad_pre, grad_stream, out1, out2, out3, out4, sums, unit_sums,
    rows, normed, scale, total, by_group,
):
    step = pl.program_id(0)

    @pl.when(step == 0)
    def _():
        rows[...] = jnp.zeros_like(rows)
        total[...] = jnp.zeros_like(total)
        receive(at[0], in1, in2, in3, in4, by_group)
        for s in range(4):
            here = slice(144 * s, 144 * s + 144)
            value = base[here] + unpack(by_group, s)
            stream[here] = value
            value, spread_of = standard(value.astype(bf16).astype(f32))
            normed[here] = value
            scale[here] = spread_of
            mixed[here] = (value * gain[...] + shift[...]).astype(bf16)

    into = group_weight(own, w_in)
    value = mm(mixed[...], into) + units[0]
    half, bell = gelu_parts(value)
    hidden[0] = (value * half).astype(bf16)
    grad = outer_cols(grad_low[...], group_weight(own_out, w_out)) * (half + value * bell)
    unit_sums[0] = jnp.sum(grad, axis=0, keepdims=True)
    grad = grad.astype(bf16)
    grad_pre[0] = grad
    total[...] += outer_cols(grad, into).astype(bf16).astype(f32)

    @pl.when(step == 3)
    def _():
        lows = []
        norm_sum = jnp.zeros((1, 768), f32)
        plain_sum = jnp.zeros((1, 768), f32)
        for s in range(4):
            here = slice(144 * s, 144 * s + 144)
            grad = total[here]
            value = normed[here]
            norm_sum += jnp.sum(grad * value, axis=0, keepdims=True)
            plain_sum += jnp.sum(grad, axis=0, keepdims=True)
            grad = grad * gain[...]
            grad = grad - jnp.mean(grad, axis=-1, keepdims=True) - value * jnp.mean(
                grad * value, axis=-1, keepdims=True
            )
            grad = widen(rows, cotangent.at[s]) + scale[here] * grad
            grad_stream[here] = grad
            lows.append(grad.astype(bf16))
        sums[0:1, :] = norm_sum
        sums[1:2, :] = plain_sum
        pack(lows, by_group)
        send(at[0], by_group, out1, out2, out3, out4)


def chain(group, base, pieces, cotangent, grad_low, gain, shift, own_in, own_out, weights, units):
    by_step = pl.BlockSpec((1, 576, 768), lambda g: (g, 0, 0))
    outs = pl.pallas_call(
        chain_kernel,
        grid=(4,),
        in_specs=[
            SMEM,
            whole((576, 768)),
            *[whole(shape) for shape in RECEIVED],
            whole((4, 3, LON, 768)),
            whole((576, 768)),
            whole((1, 768)),
            whole((1, 768)),
            whole((768, 768)),
            others_weight(0),
            whole((768, 768)),
            others_weight(1),
            pl.BlockSpec((1, 1, 768), lambda g: (g, 0, 0)),
        ],
        out_specs=[
            *[whole((576, 768))] * 2,
            by_step,
            by_step,
            whole((576, 768)),
            *[whole(piece.shape) for piece in PIECES],
            whole((2, 768)),
            pl.BlockSpec((1, 1, 768), lambda g: (g, 0, 0)),
        ],
        out_shape=[
            struct((576, 768), f32),
            struct((576, 768), bf16),
            struct((4, 576, 768), bf16),
            struct((4, 576, 768), bf16),
            struct((576, 768), f32),
            *PIECES,
            struct((2, 768), f32),
            struct((4, 1, 768), f32),
        ],
        scratch_shapes=[
            pltpu.VMEM((144, 768), f32),
            pltpu.VMEM((576, 768), f32),
            pltpu.VMEM((576, 1), f32),
            pltpu.VMEM((576, 768), f32),
            GROUPS,
        ],
        compiler_params=ROOM,
        cost_estimate=cost(14),
    )(
        group, base, *pieces, cotangent, grad_low, gain, shift, own_in, weights, own_out, weights, units
    )
    return outs[:5], outs[5:9], outs[9], outs[10]


def share_kernel(core, mixed, grad_pre, hidden, grad_low, *rest):
    own = len(rest) == 2
    out = rest[-1]

    def store(value):
        value = value.reshape(16, 1, PAD, 768)
        if own:
            value = value + rest[0][...].astype(f32)
        out[...] = value.astype(bf16)

    @pl.when(core[0] == (0 if own else 1))
    def _():
        store(inner_rows(mixed[...], grad_pre[0]))

    @pl.when(core[0] == (1 if own else 0))
    def _():
        store(inner_rows(hidden[0], grad_low[...]))


def weight_share(core, mixed, grad_pre, hidden, grad_low, *given):
    by_step = pl.BlockSpec((1, 576, 768), lambda g: (g, 0, 0))
    pieces = pl.BlockSpec((16, 1, PAD, 768), lambda g: (0, g, 0, 0))
    return pl.pallas_call(
        share_kernel,
        grid=(4,),
        in_specs=[SMEM, whole((576, 768)), by_step, by_step, whole((576, 768))] + [pieces] * len(given),
        out_specs=pieces,
        out_shape=struct((16, 4, PAD, 768), bf16),
        compiler_params=ROOM,
        cost_estimate=cost(7),
    )(core, mixed, grad_pre, hidden, grad_low, *given)


def output_kernel(hidden, own, w_out, stream, present, bias, x, grad_stream, out, sums, total, rows):
    step = pl.program_id(0)
    part = mm(hidden[0], group_weight(own, w_out)).astype(bf16).astype(f32)

    @pl.when(step == 0)
    def _():
        total[...] = part

    @pl.when(step > 0)
    def _():
        total[...] += part

    @pl.when(step == 3)
    def _():
        rows[...] = jnp.zeros_like(rows)
        norm_sum = jnp.zeros((1, 768), f32)
        plain_sum = jnp.zeros((1, 768), f32)
        for s in range(4):
            here = slice(144 * s, 144 * s + 144)
            value = stream[here] + present[here] * (total[here] + bias[...])
            for i in range(3):
                out[s, i] = value[PAD * i : PAD * i + LON].astype(bf16)
            normed, _ = standard(widen(rows, x.at[s]))
            grad = grad_stream[here] * present[here]
            norm_sum += jnp.sum(grad * normed, axis=0, keepdims=True)
            plain_sum += jnp.sum(grad, axis=0, keepdims=True)
        sums[0:1, :] = norm_sum
        sums[1:2, :] = plain_sum


def layer_output(hidden, own, weights, stream, present, bias, x, grad_stream):
    return pl.pallas_call(
        output_kernel,
        grid=(4,),
        in_specs=[
            pl.BlockSpec((1, 576, 768), lambda g: (g, 0, 0)),
            whole((768, 768)),
            others_weight(1),
            whole((576, 768)),
            whole((576, 1)),
            whole((1, 768)),
            whole((4, 3, LON, 768)),
            whole((576, 768)),
        ],
        out_specs=[whole((4, 3, LON, 768)), whole((2, 768))],
        out_shape=[struct((4, 3, LON, 768), bf16), struct((2, 768), f32)],
        scratch_shapes=[pltpu.VMEM((576, 768), f32), pltpu.VMEM((144, 768), f32)],
        compiler_params=ROOM,
        cost_estimate=cost(10),
    )(hidden, own, weights, stream, present, bias, x, grad_stream)


def final_kernel(group, x, present, grad_stream, gain, first, second, third, fourth, out, rows, by_group):
    rows[...] = jnp.zeros_like(rows)
    receive(group[0], first, second, third, fourth, by_group)
    for s in range(4):
        here = slice(144 * s, 144 * s + 144)
        normed, scale = standard(widen(rows, x.at[s]))
        stream = grad_stream[here]
        grad = (unpack(by_group, s) + stream) * present[here] * gain[...]
        grad = grad - jnp.mean(grad, axis=-1, keepdims=True) - normed * jnp.mean(
            grad * normed, axis=-1, keepdims=True
        )
        grad = stream + scale * grad
        for i in range(3):
            out[s, i] = grad[PAD * i : PAD * i + LON]


def input_grads(group, x, present, grad_stream, gain, pieces):
    return pl.pallas_call(
        final_kernel,
        in_specs=[SMEM] + [VMEM] * 8,
        out_shape=struct((4, 3, LON, 768), f32),
        scratch_shapes=[pltpu.VMEM((144, 768), f32), GROUPS],
        compiler_params=ROOM,
        cost_estimate=cost(20),
    )(group, x, present, grad_stream, gain, *pieces)


def near_kernel(*refs):
    rows = [ref[...].astype(f32) for ref in refs[:4]]
    small = [ref[...].astype(f32) for ref in refs[4:8]]
    value = jnp.concatenate(
        [rows[0] + rows[1] + rows[2] + rows[3]]
        + [(small[0] + small[1] + small[2] + small[3])[:6]]
        + [row[6:7] for row in small]
        + [row[7:11] for row in small]
        + [jnp.zeros((6, 768), f32)],
        axis=0,
    )
    refs[8][...] = value.astype(bf16)


def by_distance(rows):
    return [rows[0]] + [shifted(rows[d], 4 - d) for d in (1, 2, 3)]


def over_groups(share, small):
    return pl.pallas_call(
        near_kernel,
        out_shape=struct((80, 768), bf16),
        compiler_params=ROOM,
        cost_estimate=cost(1),
    )(*share, *small)


def copies_kernel(one, other, out):
    value = (one[...].astype(f32) + other[...].astype(f32)).astype(bf16)
    for q in range(16):
        out[q] = value


def over_snapshots(rows):
    return pl.pallas_call(
        copies_kernel,
        out_shape=struct((16,) + rows.shape, bf16),
        compiler_params=ROOM,
        cost_estimate=cost(1),
    )(rows, lax.ppermute(rows, "dp", [(0, 1), (1, 0)]))


def finish_kernel(at, own, other, w_in, w_out, f_in, f_out, small, biases, joined):
    core, group = at[0], at[1]
    own_rest = own[:, PAD:].astype(f32)
    other_rest = other[:, PAD:].astype(f32)

    for k, (zero, one) in enumerate(((own_rest, other_rest), (other_rest, own_rest))):

        @pl.when(core == k)
        def _():
            (w_in, w_out)[k][...] = own[:, :PAD].reshape(768, 768).astype(f32)
            (w_in, w_out)[1 - k][...] = other[:, :PAD].reshape(768, 768).astype(f32)
            for d in range(4):
                joined[d, :, :4] = zero[:, 10 + 4 * d : 14 + 4 * d]
                joined[d, :, 4:] = one[:, 10 + 4 * d : 14 + 4 * d]

    sums = jnp.sum(own_rest + other_rest, axis=0)
    for d in range(4):
        m = (group + d) % 4
        rows = joined[d].reshape(128, 768)
        biases[pl.ds(m, 1), :] = sums[6 + d : 7 + d]
        for which, out in enumerate((f_in, f_out)):
            for part in range(2):
                for b in range(2):
                    pieces = []
                    for piece in range(3):
                        row = which * 384 + part * 192 + b * 96 + piece * 32
                        u, row = row // 128, row % 128
                        pieces.append(rows[row : row + 32, 128 * u : 128 * u + 128])
                    out[part, 2 * m + b] = jnp.concatenate(pieces, axis=0)[:, :96]
    small[...] = sums[:8]


def finish(at, *rows):
    return pl.pallas_call(
        finish_kernel,
        in_specs=[SMEM] + [VMEM] * 2,
        out_shape=[
            struct((768, 768), f32),
            struct((768, 768), f32),
            struct((2, 8, 96, 96), f32),
            struct((2, 8, 96, 96), f32),
            struct((8, 768), f32),
            struct((4, 768), f32),
        ],
        scratch_shapes=[pltpu.VMEM((4, 16, 8, 768), f32)],
        compiler_params=ROOM,
        cost_estimate=cost(5),
    )(at, *rows)


def swap(value, axes):
    return lax.all_to_all(value, axes, 0, 0, tiled=True)


def across(columns):
    return swap(columns.reshape(32, 24, 768), WIDE).reshape(768, 768)


def after(value, *others):
    return lax.optimization_barrier((value,) + others)[0]


def shards(
    inputs,
    validity,
    gain_first,
    shift_first,
    spectral_in,
    spectral_in_bias,
    spectral_out,
    spectral_out_bias,
    gain_second,
    shift_second,
    weight_in,
    bias_in,
    weight_out,
    bias_out,
    cotangent,
):
    core = lax.axis_index("core")
    group = lax.axis_index("mlp")
    table = {name: jnp.asarray(value) for name, value in tables().items()}
    mask, fold = (jnp.asarray(value) for value in block_fold())
    gain_first, shift_first, gain_second, shift_second, bias_out = (
        value.reshape(1, 768)
        for value in (gain_first, shift_first, gain_second, shift_second, bias_out)
    )

    present = jnp.pad(validity.astype(f32), ((0, 0), (0, 0), (0, PAD - LON))).reshape(576, 1)
    here = group.astype(jnp.int32).reshape(1)
    lanes = jnp.pad(validity.astype(f32).reshape(12, LON), ((0, 0), (0, PAD - LON)))
    tokens = exchange(*norm_pack(here, inputs, present, lanes, gain_first, shift_first))

    wide = lax.axis_index(WIDE)
    high = lax.reduce_precision(bias_in, 8, 7)
    middle = lax.reduce_precision(bias_in - high, 8, 7)
    bias_rows = jnp.stack([high, middle, bias_in - high - middle]).astype(bf16)
    both = jnp.concatenate([weight_in, weight_out], axis=0)
    piece = jnp.concatenate(
        [
            lax.dynamic_slice_in_dim(both, wide * PAD, PAD, 0),
            bias_rows,
            jnp.zeros((5, 768), bf16),
        ]
    )
    pieces = jnp.stack([piece] + [shifted(piece, d) for d in (1, 2, 3)])
    weights = lax.all_gather(pieces[1:, :PAD], WIDE)
    units = pieces[:, PAD : PAD + 3].astype(f32)
    units = (units[:, 0] + units[:, 1] + units[:, 2]).reshape(4, 1, 768)

    mix_in, mix_out = mixers(spectral_in, spectral_out, mask)
    mix_in_bias, mix_out_bias = (
        jnp.tile(value.reshape(2, 1, 192), (1, 2, 1)).reshape(1, 768)
        for value in (spectral_in_bias, spectral_out_bias)
    )

    columns, kept = to_columns_and_keep(here, table["lon_fwd"], tokens)
    columns = across(columns)
    row_validity = whole_validity(kept)
    back, low, first, active, second = filter_forward(
        columns, table["grid_fwd"], table["grid_inv"], mix_in, mix_out, mix_in_bias, mix_out_bias
    )
    filtered = exchange(*to_pieces(here, table["lon_inv"], across(back)))
    base, grad_low, bias_sum = prepare(inputs, present, cotangent, gain_first, shift_first)
    (stream, mixed, hidden, grad_pre, grad_stream), sent, sums, unit_sums = chain(
        here,
        base,
        filtered,
        cotangent,
        grad_low,
        gain_second,
        shift_second,
        weight_in,
        weight_out,
        weights,
        units,
    )
    operands = (core.astype(jnp.int32).reshape(1), mixed, grad_pre, hidden, grad_low)
    share = weight_share(*operands)
    share = weight_share(*operands, lax.ppermute(share, "core", [(0, 1), (1, 0)]))
    output, first_sums = layer_output(
        hidden, weight_out, weights, after(stream, share), present, bias_out, inputs, grad_stream
    )
    share = lax.psum_scatter(share.reshape(3072, 768), XY, scatter_dimension=0, tiled=True)

    columns = after(across(to_columns(here, table["lon_inv_t"], exchange(*sent))), output)
    back, filter_sums = filter_backward(
        columns,
        table["grid_inv_t"],
        table["grid_fwd_t"],
        mix_in,
        mix_out,
        low,
        first,
        active,
        second,
        mask,
        fold,
        table["place"],
    )
    back = across(back)
    filter_share = jnp.sum(back.reshape(32, 24, 768)[:, 18:22].astype(f32), axis=0).astype(bf16)
    sent, piece_sums = to_pieces_and_sums(
        here, table["lon_fwd_t"], back, kept, row_validity, gain_first, shift_first
    )
    grad_inputs = input_grads(here, inputs, present, grad_stream, gain_first, exchange(*sent))

    filter_sums = jnp.sum(filter_sums.reshape(2, 2, 2, 192), axis=2).reshape(1, 768)
    rest = jnp.concatenate([first_sums + piece_sums, sums, bias_sum, filter_sums]).astype(bf16)
    rest = jnp.concatenate([rest, filter_share, jnp.zeros((5, 768), bf16)])
    unit_sums = unit_sums.reshape(4, 1, 768).astype(bf16)
    rest = [jnp.concatenate([unit_sums[d], rest]) for d in range(4)]
    rest = by_distance(rest)
    share = after(share, *rest[1:]).reshape(4, PAD, 768)
    rows = over_groups(by_distance([share[d] for d in range(4)]), rest)
    rows = swap(over_snapshots(rows), XY)
    grad_w_in, grad_w_out, grad_f_in, grad_f_out, small, biases = finish(
        jnp.stack([core, group]).astype(jnp.int32),
        rows,
        lax.ppermute(rows, "core", [(0, 1), (1, 0)]),
    )
    biases = biases.reshape(4, 2, 2, 2, 96).transpose(1, 2, 0, 3, 4).reshape(2, 2, 8, 96)
    mine = lax.dynamic_slice_in_dim(small[1:6], group * 192, 192, 1)
    return (
        output,
        grad_inputs,
        mine[0],
        mine[1],
        grad_f_in,
        biases[0],
        grad_f_out,
        biases[1],
        mine[2],
        mine[3],
        grad_w_in,
        small[0],
        grad_w_out,
        mine[4],
    )


def solution(mesh):
    fine = Mesh(mesh.devices.reshape(2, 4, 4, 2, 4), EVERY)
    tokens = P("dp", ("x", "y", "core"), "mlp")
    placed = (
        tokens,
        tokens,
        P(),
        P(),
        P(None, "mlp"),
        P(None, "mlp"),
        P(None, "mlp"),
        P(None, "mlp"),
        P(),
        P(),
        P(None, "mlp"),
        P("mlp"),
        P("mlp", None),
        P(),
        tokens,
    )
    return jax.shard_map(
        shards,
        mesh=fine,
        in_specs=placed,
        out_specs=(
            tokens,
            tokens,
            P("mlp"),
            P("mlp"),
            P(),
            P(),
            P(),
            P(),
            P("mlp"),
            P("mlp"),
            P(None, "mlp"),
            P("mlp"),
            P("mlp", None),
            P("mlp"),
        ),
        check_vma=False,
    )
```
